32 devices in a mesh: section: 4 (over z), dp: 2 (over core), tensor: 4 (over y, x).
Axes of the slice: x: 2, y: 2, z: 4, core: 2. Of those that a mesh axis runs over, the one named last changes fastest.
Arguments:
- patches: bfloat16 [6144, 1280], P(('section', 'dp')), may hold values from -6 to 6
- window_ids: int32 [6144], P(('section', 'dp')), may hold values from 0 to 152, never falling along the last dimension, each value on 1 to 64 neighbouring positions
- norm_gain: float32 [1280], replicated, may hold values from 0.25 to 1.75
- w_qkv: bfloat16 [1280, 3, 1280], P(('section', 'dp'), None, 'tensor'), may hold values from -0.15625 to 0.15625
- qkv_bias: float32 [3, 1280], P(None, 'tensor'), may hold values from -10 to 10
- w_out: bfloat16 [1280, 1280], P(('section', 'dp'), 'tensor'), may hold values from -0.15625 to 0.15625
Outputs:
- mixed: bfloat16 [6144, 1280], P(('section', 'dp'))
The draws below stay inside these ranges and needn't reach their ends.
Inputs may be any that keep to these rules, and one draw needn't show every extreme that they name: window_ids never fall along the packed order; each window holds 1 to 64 consecutive patches, and some window holds exactly 64.
All inputs are finite; a program needn't handle non-finite values.
Results may differ from the reference program's by a relative error of at most 0.012.
Values may be sent and summed in bfloat16 or wider, within the bound.
A program may use at most 64 MiB of HBM per device.

```python
import math
import jax
import jax.numpy as jnp
import numpy as np
from jax import lax

D = 1280
HEADS = 16
HEAD = 80
WIN = 64
PATCHES = 6144


def draw_qkv_bias(key, part):
    base = jax.random.normal(jax.random.fold_in(key, 1), (3, D), jnp.float32) * 0.5
    base = jnp.clip(base, -3.0, 3.0)
    return base


def levels(stream_key, extent, shards, smallest, high):
    def one(axis_at, parts):
        draws = jax.random.uniform(jax.random.fold_in(jax.random.fold_in(stream_key, 6), axis_at), (parts,), jnp.float32, smallest / len(shards), high / len(shards))
        return jnp.repeat(jnp.exp(draws), extent[axis_at] // parts).reshape((-1,) + (1,) * (len(extent) - axis_at - 1))

    gain = one(*shards[0])
    for cut in shards[1:]:
        gain = gain * one(*cut)
    return gain


def length_profile(amount, total, bound, skew):
    weights = [(1 << 20) // math.isqrt(rank ** skew) + 1 for rank in range(2, amount + 1)]
    rest, given = total - bound - (amount - 1), [1] * (amount - 1)
    while rest > 0:
        free = [i for i in range(amount - 1) if given[i] < bound]
        whole, left = sum([weights[i] for i in free]), rest
        for i in free:
            addition = min(bound - given[i], max(1, left * weights[i] // whole), rest)
            given[i] = given[i] + addition
            rest = rest - addition
    return np.array([bound] + given)


def uneven_parts(key, amount, total, most, slope):
    if amount == 2:
        one = jax.random.randint(key, (), max(1, total - most), min(most, total - 1) + 1)
        return jnp.stack([one, total - one])
    tallies = jnp.asarray(length_profile(amount, total, most, slope), jnp.int32)
    twos = (amount - 1) // 2
    giver, taker = tallies[1:1 + 2 * twos:2], tallies[2:2 + 2 * twos:2]
    room = jnp.minimum(giver - 1, most - taker)
    passed = jax.random.randint(jax.random.fold_in(key, 1), (twos,), 0, 1 << 20) % (room + 1)
    tallies = tallies.at[1:1 + 2 * twos:2].set(giver - passed).at[2:2 + 2 * twos:2].set(taker + passed)
    return tallies[jax.random.permutation(jax.random.fold_in(key, 2), amount)]


def bell_draw(stream_key, shape, width, bound, cuts=(), kind=jnp.bfloat16):
    gain = levels(stream_key, shape, cuts, -0.22, 0.18) if cuts else 1.0
    drawn = jax.random.normal(stream_key, shape, jnp.float32) * width * gain
    return jnp.minimum(jnp.maximum(drawn, -bound), bound).astype(kind)


def setup_inputs(seed: int = 0) -> dict:
    streams_of = jax.random.split(jax.random.key(seed), 7)
    patches = bell_draw(streams_of[0], (PATCHES, D), 1.0, 6.0, ((0, 8),))
    window_ids = jnp.searchsorted(jnp.cumsum(uneven_parts(streams_of[1], PATCHES // 40, PATCHES, WIN, 1)), jnp.arange(PATCHES), side="right").astype(jnp.int32)
    norm_gain = jnp.clip(1.0 + 0.15 * jax.random.normal(streams_of[2], (D,), jnp.float32), 0.25, 1.75)
    w_qkv = bell_draw(streams_of[3], (D, 3, D), D ** -0.5, 0.15625, ((0, 8), (2, 4)))
    qkv_bias = draw_qkv_bias(jax.random.fold_in(streams_of[6], 71), 0)
    w_out = bell_draw(streams_of[5], (D, D), D ** -0.5, 0.15625, ((0, 8), (1, 4)))
    return dict(patches=patches, window_ids=window_ids, norm_gain=norm_gain, w_qkv=w_qkv, qkv_bias=qkv_bias, w_out=w_out)


def reference(patches, window_ids, norm_gain, w_qkv, qkv_bias, w_out):
    values_f = patches.astype(jnp.float32)
    scale_row = lax.rsqrt(lax.optimization_barrier(jnp.mean(values_f * values_f, axis=-1, keepdims=True)) + 1e-06)
    normed = (values_f * scale_row * norm_gain).astype(jnp.bfloat16)
    proj = jnp.dot(normed, w_qkv.reshape(D, 3 * D), preferred_element_type=jnp.float32)
    proj = (proj + qkv_bias.reshape(3 * D)).astype(jnp.bfloat16)
    queries = proj[:, :D]
    keyvals = jnp.pad(proj[:, D:], ((WIN, WIN), (0, 0)))
    marks = jnp.pad(window_ids + 1, (WIN, WIN))
    block = 512
    factor = 1.0 / HEAD ** 0.5

    def one_block(index):
        start = (index * block).astype(jnp.int32)
        qblock = lax.dynamic_slice_in_dim(queries, start, block, 0).astype(jnp.float32).reshape(block, HEADS, HEAD)
        kvblock = lax.dynamic_slice_in_dim(keyvals, start, block + 2 * WIN, 0).astype(jnp.float32)
        kblock = kvblock[:, :D].reshape(block + 2 * WIN, HEADS, HEAD)
        vblock = kvblock[:, D:].reshape(block + 2 * WIN, HEADS, HEAD)
        mark_q = lax.dynamic_slice_in_dim(marks, start + WIN, block, 0)
        mark_k = lax.dynamic_slice_in_dim(marks, start, block + 2 * WIN, 0)
        allowed = mark_q[:, None] == mark_k[None, :]
        scores = jnp.einsum('qhd,khd->hqk', qblock, kblock) * factor
        scores = jnp.where(allowed[None], scores, jnp.float32(-1e+30))
        top = lax.optimization_barrier(jnp.max(scores, axis=-1, keepdims=True))
        expo = jnp.where(allowed[None], jnp.exp(scores - top), jnp.float32(0.0))
        probs = (expo / lax.optimization_barrier(jnp.sum(expo, axis=-1, keepdims=True))).astype(jnp.bfloat16)
        probs = lax.optimization_barrier(probs).astype(jnp.float32)
        result = jnp.einsum('hqk,khd->qhd', probs, vblock)
        return result.reshape(block, D).astype(jnp.bfloat16)
    attn = lax.map(one_block, jnp.arange(PATCHES // block, dtype=jnp.int32)).reshape(PATCHES, D)
    projected = lax.dot_general(attn, w_out, (((1,), (1,)), ((), ())), preferred_element_type=jnp.float32)
    total = values_f + projected
    return total.astype(jnp.bfloat16)
```

```python
import functools
import math

import jax
import jax.numpy as jnp
from jax import lax
from jax.experimental import pallas as pl
from jax.experimental.pallas import tpu as pltpu
from jax.sharding import PartitionSpec as P

HEAD = 80
WIN = 64
MESH = pl.DeviceIdType.MESH


def with_halo(cells, sides, width):
    for axis, dim in sides:
        count = lax.axis_size(axis)
        ends = count - 1
        head = lax.slice_in_dim(cells, 0, width, axis=dim)
        tail = lax.slice_in_dim(cells, cells.shape[dim] - width, cells.shape[dim], axis=dim)
        cells = jnp.concatenate(
            [
                lax.ppermute(tail, axis, [(i, (i + 1) % count) for i in range(ends)]),
                cells,
                lax.ppermute(head, axis, [((i + 1) % count, i) for i in range(ends)]),
            ],
            axis=dim,
        )
    return cells


def local(patches, window_ids, norm_gain, w_qkv, qkv_bias, w_out):
    rows = patches.shape[0]
    local_cols = w_qkv.shape[2]
    local_heads = local_cols // HEAD
    values_f = patches.astype(jnp.float32)
    scale_row = lax.rsqrt(jnp.mean(values_f * values_f, axis=-1, keepdims=True) + 1e-06)
    normed = (values_f * scale_row * norm_gain).astype(jnp.bfloat16)
    piece = lax.all_gather(w_qkv, ("section", "dp"), axis=0, tiled=True)
    count = piece.shape[0]
    proj = jnp.dot(normed, piece.reshape(count, 3 * local_cols), preferred_element_type=jnp.float32)
    proj = (proj + qkv_bias.reshape(3 * local_cols)).astype(jnp.bfloat16)
    keyvals = with_halo(proj[:, local_cols:], ((("section", "dp"), 0),), WIN)
    marks = with_halo(window_ids + 1, ((("section", "dp"), 0),), WIN)
    block_rows = 128
    blocks = rows // block_rows
    key_span = block_rows + 2 * WIN
    queries = proj[:, :local_cols].reshape(blocks, block_rows, local_heads, HEAD)
    kv_blocks = jnp.stack(
        [keyvals[i * block_rows : i * block_rows + key_span] for i in range(blocks)]
    )
    mark_blocks = jnp.stack(
        [marks[i * block_rows : i * block_rows + key_span] for i in range(blocks)]
    )
    keys = kv_blocks[:, :, :local_cols].reshape(blocks, key_span, local_heads, HEAD)
    vals = kv_blocks[:, :, local_cols:].reshape(blocks, key_span, local_heads, HEAD)
    mark_q = marks[WIN : WIN + rows].reshape(blocks, block_rows)
    allowed = mark_q[:, :, None] == mark_blocks[:, None, :]
    factor = 1.0 / HEAD**0.5
    scores = (
        jnp.einsum("bqhd,bkhd->bhqk", queries, keys, preferred_element_type=jnp.float32) * factor
    )
    scores = jnp.where(allowed[:, None], scores, jnp.float32(-1e30))
    top = jnp.max(scores, axis=-1, keepdims=True)
    expo = jnp.where(allowed[:, None], jnp.exp(scores - top), jnp.float32(0.0))
    probs = (expo / jnp.sum(expo, axis=-1, keepdims=True)).astype(jnp.bfloat16)
    attn = jnp.einsum("bhqk,bkhd->bqhd", probs, vals, preferred_element_type=jnp.float32)
    attn = attn.reshape(rows, local_cols).astype(jnp.bfloat16)
    partial_out = lax.dot_general(
        attn,
        lax.all_gather(w_out, ("section", "dp"), axis=0, tiled=True),
        (((1,), (1,)), ((), ())),
        preferred_element_type=jnp.float32,
    )
    summed = lax.psum(partial_out.astype(jnp.bfloat16), "tensor").astype(jnp.float32)
    return (values_f + summed).astype(jnp.bfloat16)


def flip(x):
    return pltpu.roll(x.astype(jnp.float32), 64, 1).astype(x.dtype)


def kernel(
    sections,
    x_ref, ids_ref, gain_ref, pack_ref, bias_ref, out_ref,
    wp, normed, acc, q3, kv3, attn, wo, wof, idb, kid,
    up_s, dn_s, sib_s, wp_r, wx_s, wy_s, wf_s, w_r, ws_s, ws_r,
    id_s, id_r, h_s, h_r, ax_s, ay_s, af_s, a_r,
):
    rows, width = x_ref.shape
    depth = width // (2 * sections)
    halfd = depth // 2
    wq_rows = 7 * depth + halfd
    blocks = rows // 128
    last = sections - 1
    s, c, t = lax.axis_index("section"), lax.axis_index("dp"), lax.axis_index("tensor")
    oc = 1 - c
    tx = t + 1 - 2 * (t % 2)
    ty = (t + 2) % 4
    td = (tx + 2) % 4
    up, dn, sib = (s + 1, c, t), (s - 1, c, t), (s, oc, t)
    xn, yn = (s, c, tx), (s, c, ty)
    hz = s - 1 + 2 * c
    hdev = (hz, oc, t)
    has_up, has_dn = s < last, s > 0
    has_h = jnp.logical_and(hz >= 0, hz <= last)

    def rc(src, dst, ss, rs, dev):
        return pltpu.make_async_remote_copy(
            src_ref=src, dst_ref=dst, send_sem=ss, recv_sem=rs, device_id=dev, device_id_type=MESH
        )

    barrier = pltpu.get_barrier_semaphore()

    def greet(dev):
        pl.semaphore_signal(barrier, inc=1, device_id=dev, device_id_type=MESH)

    greet(sib)
    greet(xn)
    greet(yn)

    @pl.when(has_up)
    def _():
        greet(up)

    @pl.when(has_dn)
    def _():
        greet(dn)

    @pl.when(has_h)
    def _():
        greet(hdev)

    peers = 3 + has_up.astype(jnp.int32) + has_dn.astype(jnp.int32) + has_h.astype(jnp.int32)
    pl.semaphore_wait(barrier, peers)

    def src_of(j, own):
        return pack_ref if own else wp.at[2 * j + c]

    def d_up(j, own=False):
        return rc(src_of(j, own), wp.at[2 * j + c], up_s.at[j], wp_r.at[2 * j + c], up)

    def d_dn(j, own=False):
        return rc(src_of(j, own), wp.at[2 * j + c], dn_s.at[j], wp_r.at[2 * j + c], dn)

    def d_sib(j, own=False):
        return rc(src_of(j, own), wp.at[2 * j + c], sib_s.at[j], wp_r.at[2 * j + c], sib)

    def got(j, parity):
        g = 2 * j + parity
        rc(wp.at[g], wp.at[g], sib_s.at[j], wp_r.at[g], sib).wait_recv()

    def wo_src(j, own):
        return src_of(j, own).at[pl.ds(wq_rows, 2 * depth + halfd)]

    def d_wx(j, own=False):
        return rc(wo_src(j, own), wo.at[c, 0, j], wx_s.at[j], w_r.at[0, j], xn)

    def d_wy(j, own=False):
        return rc(wo_src(j, own), wo.at[c, 1, j], wy_s.at[j], w_r.at[1, j], yn)

    def d_fx(j):
        return rc(wo.at[c, 0, j], wo.at[c, 2, j], wf_s.at[j], w_r.at[2, j], yn)

    def d_fy(j):
        return rc(wo.at[c, 1, j], wo.at[c, 2, j], wf_s.at[j], w_r.at[2, j], xn)

    def d_ws():
        return rc(wo.at[c], wo.at[c], ws_s, ws_r, sib)

    d_wos = (d_wx, d_wy)

    @pl.when(has_up)
    def _():
        d_up(s, True).start()

    @pl.when(has_dn)
    def _():
        d_dn(s, True).start()

    d_sib(s, True).start()
    for d in d_wos:
        d(s, True).start()

    def d_id(k):
        return functools.partial(rc, ids_ref, idb.at[2 - 2 * k], id_s.at[k], id_r.at[1 - k])

    @pl.when(c == 0)
    def _():
        d_id(1)(sib).start()

        @pl.when(has_h)
        def _():
            d_id(0)(hdev).start()

    @pl.when(c == 1)
    def _():
        d_id(0)(sib).start()

        @pl.when(has_h)
        def _():
            d_id(1)(hdev).start()

    def norm_block(i, _):
        r = pl.ds(pl.multiple_of(i * 128, 128), 128)
        v = x_ref[r, :].astype(jnp.float32)
        sc = lax.rsqrt(jnp.mean(v * v, axis=-1, keepdims=True) + 1e-06)
        n = v * sc * gain_ref[...]
        for g in range(2 * sections):
            normed[g, r, :] = n[:, g * depth : (g + 1) * depth].astype(jnp.bfloat16)
        acc[r, :] = jnp.broadcast_to(bias_ref[...], (128, 1024))
        return 0

    lax.fori_loop(0, blocks, norm_block, 0)

    def mm(ref, g):
        a = normed[g]
        for p in range(4):
            lo = ref[pl.ds(2 * p * depth, depth), :]
            if p < 3:
                hi = ref[pl.ds((2 * p + 1) * depth, depth), :]
            else:
                h = ref[pl.ds(7 * depth, halfd), :]
                hi = jnp.concatenate([h, flip(h)], axis=0)
            w = jnp.concatenate([lo, hi], axis=1)
            acc[:, 256 * p : 256 * p + 256] += jnp.dot(a, w, preferred_element_type=jnp.float32)

    def spread(j):
        rc(wo.at[c, 0, j], wo.at[c, 0, j], wx_s.at[j], w_r.at[0, j], xn).wait_recv()
        rc(wo.at[c, 1, j], wo.at[c, 1, j], wy_s.at[j], w_r.at[1, j], yn).wait_recv()

        @pl.when(j % 2 == 0)
        def _():
            d_fx(j).start()

        @pl.when(j % 2 == 1)
        def _():
            d_fy(j).start()

    mm(pack_ref, 2 * s + c)
    got(s, oc)
    mm(wp.at[2 * s + oc], 2 * s + oc)
    spread(s)

    def step(d, _):
        jb, ja = s - d, s + d

        @pl.when(jb >= 0)
        def _():
            got(jb, c)

            @pl.when(has_up)
            def _():
                d_up(jb).start()

            d_sib(jb).start()
            for e in d_wos:
                e(jb).start()

        @pl.when(ja <= last)
        def _():
            got(ja, c)

            @pl.when(has_dn)
            def _():
                d_dn(ja).start()

            d_sib(ja).start()
            for e in d_wos:
                e(ja).start()

        for k in range(2):
            j = s - d + 2 * d * k

            @pl.when(jnp.logical_and(j >= 0, j <= last))
            def _():
                def core(m, _):
                    g = 2 * j + lax.rem(c + m, 2)

                    @pl.when(m == 1)
                    def _():
                        got(j, oc)

                    mm(wp.at[g], g)
                    return 0

                lax.fori_loop(0, 2, core, 0)
                spread(j)

        return 0

    lax.fori_loop(1, sections, step, 0)

    def settle(i, _):
        r = pl.ds(pl.multiple_of(i * 128, 128), 128)
        rk = pl.ds(pl.multiple_of(i * 128 + WIN, WIN), 128)
        p = acc[r, :].astype(jnp.bfloat16)
        q3[r, 0:256] = p[:, 0:256]
        q3[r, 256:384] = p[:, 768:896]
        kv3[rk, 0:256] = p[:, 256:512]
        kv3[rk, 256:384] = p[:, 896:1024]
        kv3[rk, 384:640] = p[:, 512:768]
        kv3[rk, 640:768] = p[:, 768:896]
        return 0

    lax.fori_loop(0, blocks, settle, 0)

    def d_h(k):
        src = kv3.at[pl.ds(WIN if k == 0 else rows, WIN)]
        dst = kv3.at[pl.ds(rows + WIN if k == 0 else 0, WIN)]
        return functools.partial(rc, src, dst, h_s.at[k], h_r.at[1 - k])

    @pl.when(c == 0)
    def _():
        d_h(1)(sib).start()

        @pl.when(has_h)
        def _():
            d_h(0)(hdev).start()

        @pl.when(jnp.logical_not(has_h))
        def _():
            kv3[0:WIN, :] = jnp.zeros((WIN, 768), jnp.bfloat16)
            idb[0] = jnp.full((8, 128), -1, jnp.int32)

    @pl.when(c == 1)
    def _():
        d_h(0)(sib).start()

        @pl.when(has_h)
        def _():
            d_h(1)(hdev).start()

        @pl.when(jnp.logical_not(has_h))
        def _():
            kv3[rows + WIN : rows + 2 * WIN, :] = jnp.zeros((WIN, 768), jnp.bfloat16)
            idb[2] = jnp.full((8, 128), -1, jnp.int32)

    def wait_side(d, k):
        @pl.when(jnp.logical_or(c == 1 - k, has_h))
        def _():
            d(1 - k)(sib).wait_recv()

    wait_side(d_id, 0)
    wait_side(d_id, 1)
    chain = jnp.concatenate([idb[0, blocks - 1 : blocks], ids_ref[0:blocks, :], idb[2, 0:1]], axis=0)
    lane8 = lax.broadcasted_iota(jnp.int32, (8, 128), 1)
    after = jnp.concatenate([chain[1:], chain[:1]], axis=0)
    kid[...] = pltpu.roll(jnp.where(lane8 < 64, after, chain), 64, 1)

    lane = lax.broadcasted_iota(jnp.int32, (128, 128), 1)
    scale = math.log2(math.e) / HEAD**0.5
    zero = jnp.zeros((128, 128), jnp.bfloat16)

    def d_ax(b):
        r = pl.ds(pl.multiple_of(b * 128, 128), 128)
        return rc(attn.at[t, r], attn.at[t, r], ax_s.at[b], a_r.at[0, b], xn)

    def d_ay(b):
        r = pl.ds(pl.multiple_of(b * 128, 128), 128)
        return rc(attn.at[t, r], attn.at[t, r], ay_s.at[b], a_r.at[1, b], yn)

    def d_afx(b):
        r = pl.ds(pl.multiple_of(b * 128, 128), 128)
        return rc(attn.at[tx, r], attn.at[tx, r], af_s.at[b], a_r.at[2, b], yn)

    def d_afy(b):
        r = pl.ds(pl.multiple_of(b * 128, 128), 128)
        return rc(attn.at[ty, r], attn.at[ty, r], af_s.at[b], a_r.at[2, b], xn)

    def attend(b):
        r = pl.ds(pl.multiple_of(b * 128, 128), 128)
        rk = pl.ds(pl.multiple_of(b * 128, 128), 256)
        idq = jnp.transpose(jnp.broadcast_to(ids_ref[pl.ds(b, 1), :], (128, 128)))
        ok = jnp.concatenate([idq == kid[pl.ds(b, 1), :], idq == kid[pl.ds(b + 1, 1), :]], axis=1)
        qa, qb, qh = q3[r, 0:128], q3[r, 128:256], q3[r, 256:384]
        parts = (
            (jnp.where(lane < 80, qa, zero), 0, 128),
            (
                jnp.concatenate(
                    [jnp.where(lane >= 80, qa, zero), jnp.where(lane < 32, qb, zero)], axis=1
                ),
                0,
                256,
            ),
            (jnp.where(jnp.logical_and(lane >= 32, lane < 112), qb, zero), 128, 256),
            (
                jnp.concatenate(
                    [jnp.where(lane >= 112, qb, zero), jnp.where(lane < 64, qh, zero)], axis=1
                ),
                128,
                384,
            ),
        )
        outs = []
        for q, lo, hi in parts:
            sc = lax.dot_general(
                q, kv3[rk, lo:hi], (((1,), (1,)), ((), ())), preferred_element_type=jnp.float32
            )
            sc = jnp.where(ok, sc, jnp.float32(-1e30))
            top = jnp.max(sc, axis=-1, keepdims=True)
            e = jnp.exp2((sc - top) * scale)
            total = jnp.sum(e, axis=-1, keepdims=True)
            o = jnp.dot(
                e.astype(jnp.bfloat16), kv3[rk, 384 + lo : 384 + hi], preferred_element_type=jnp.float32
            )
            outs.append(o * (1.0 / total))
        o0, o1, o2, o3 = outs
        attn[t, r, 0:128] = jnp.where(lane < 80, o0, o1[:, :128]).astype(jnp.bfloat16)
        attn[t, r, 128:256] = jnp.where(
            lane < 32, o1[:, 128:], jnp.where(lane < 112, o2, o3[:, :128])
        ).astype(jnp.bfloat16)
        attn[t, r, 256:384] = jnp.where(lane >= 64, o3[:, 128:], jnp.float32(0.0)).astype(jnp.bfloat16)
        d_ax(b).start()
        d_ay(b).start()

    def relay(b):
        r = pl.ds(pl.multiple_of(b * 128, 128), 128)
        rc(attn.at[tx, r], attn.at[tx, r], ax_s.at[b], a_r.at[0, b], xn).wait_recv()
        rc(attn.at[ty, r], attn.at[ty, r], ay_s.at[b], a_r.at[1, b], yn).wait_recv()

        @pl.when(b % 2 == 0)
        def _():
            d_afx(b).start()

        @pl.when(b % 2 == 1)
        def _():
            d_afy(b).start()

    def order(i):
        return jnp.where(i < blocks - 2, i + 1, jnp.where(i == blocks - 2, 0, blocks - 1))

    def attend_step(i, _):
        @pl.when(i == blocks - 2)
        def _():
            wait_side(d_h, 0)
            wait_side(d_h, 1)

        attend(order(i))

        @pl.when(i == 2)
        def _():
            def diag(j, _):
                rc(wo.at[c, 2, j], wo.at[c, 2, j], wf_s.at[j], w_r.at[2, j], xn).wait_recv()
                return 0

            lax.fori_loop(0, sections, diag, 0)
            d_ws().start()

        @pl.when(i >= 2)
        def _():
            relay(order(i - 2))

        return 0

    lax.fori_loop(0, blocks, attend_step, 0)

    rc(wo.at[oc], wo.at[oc], ws_s, ws_r, sib).wait_recv()

    def unpack(src, tt, g):
        base = g * depth
        wof[tt, pl.ds(pl.multiple_of(base, 16), depth), 0:128] = src[0:depth, :]
        wof[tt, pl.ds(pl.multiple_of(base, 16), depth), 128:256] = src[depth : 2 * depth, :]
        h = src[2 * depth : 2 * depth + halfd, :]
        wof[tt, pl.ds(pl.multiple_of(base, 16), halfd), 256:384] = flip(h)
        wof[tt, pl.ds(pl.multiple_of(base + halfd, 16), halfd), 256:384] = h

    def unpack_all(j, _):
        for m in range(2):
            g = 2 * j + m
            for k, tt in enumerate((tx, ty, td)):
                unpack(wo.at[m, k, j], tt, g)

            @pl.when(g != 2 * s + c)
            def _():
                unpack(wp.at[g, pl.ds(wq_rows, 2 * depth + halfd)], t, g)

        return 0

    lax.fori_loop(0, sections, unpack_all, 0)
    unpack(pack_ref.at[pl.ds(wq_rows, 2 * depth + halfd)], t, 2 * s + c)

    def project(i, _):
        @pl.when(i < 2)
        def _():
            relay(order(i + blocks - 2))

        b = order(i)
        r = pl.ds(pl.multiple_of(b * 128, 128), 128)
        rc(attn.at[td, r], attn.at[td, r], af_s.at[b], a_r.at[2, b], xn).wait_recv()
        a = jnp.concatenate([attn[k, r, :] for k in range(4)], axis=1)
        for n in range(width // 256):
            w = jnp.concatenate([wof[k, 256 * n : 256 * n + 256, :] for k in range(4)], axis=1)
            total = lax.dot_general(
                a, w, (((1,), (1,)), ((), ())), preferred_element_type=jnp.float32
            )
            cols = slice(256 * n, 256 * n + 256)
            out_ref[r, cols] = (x_ref[r, cols].astype(jnp.float32) + total).astype(jnp.bfloat16)
        return 0

    lax.fori_loop(0, blocks, project, 0)

    def sent_w(j, _):
        @pl.when(jnp.logical_and(has_up, j <= s))
        def _():
            d_up(j).wait_send()

        @pl.when(jnp.logical_and(has_dn, j >= s))
        def _():
            d_dn(j).wait_send()

        d_sib(j).wait_send()
        d_wx(j).wait_send()
        d_wy(j).wait_send()
        d_fx(j).wait_send()
        return 0

    lax.fori_loop(0, sections, sent_w, 0)
    d_ws().wait_send()

    def sent_a(b, _):
        d_ax(b).wait_send()
        d_ay(b).wait_send()
        d_afx(b).wait_send()
        return 0

    lax.fori_loop(0, blocks, sent_a, 0)
    for d in (d_id, d_h):
        for k in range(2):

            @pl.when(jnp.logical_or(c == 1 - k, has_h))
            def _():
                d(k)(sib).wait_send()


def fold(w):
    half = w.shape[0] // 2
    return jnp.concatenate([w[:half], w[half:]], axis=1)


def fused(sections, patches, window_ids, norm_gain, w_qkv, qkv_bias, w_out):
    rows, width = patches.shape
    depth = w_qkv.shape[0]
    blocks = rows // 128
    q, k, v = w_qkv[:, 0], w_qkv[:, 1], w_qkv[:, 2]
    tiles = [w[:, lo : lo + 128] for w in (q, k, v) for lo in (0, 128)]
    tiles += [jnp.concatenate([q[:, 256:], v[:, 256:]], axis=1), fold(k[:, 256:])]
    tiles += [w_out[:, :128], w_out[:, 128:256], fold(w_out[:, 256:])]
    pack = jnp.concatenate(tiles, axis=0)
    b = qkv_bias
    bias = jnp.concatenate(
        [b[0, :256], b[1, :256], b[2, :256], b[0, 256:], b[2, 256:], b[1, 256:], jnp.zeros((64,), b.dtype)]
    )[None]
    ids = jnp.pad(window_ids.reshape(blocks, 128), ((0, 8 - blocks), (0, 0)))
    bf, dma = jnp.bfloat16, pltpu.SemaphoreType.DMA
    shards = 2 * sections
    wo_rows = 2 * depth + depth // 2
    vmem = pl.BlockSpec(memory_space=pltpu.VMEM)
    return pl.pallas_call(
        functools.partial(kernel, sections),
        out_shape=jax.ShapeDtypeStruct((rows, width), bf),
        in_specs=[vmem] * 5,
        out_specs=vmem,
        scratch_shapes=[
            pltpu.VMEM((shards, 10 * depth, 128), bf),
            pltpu.VMEM((shards, rows, depth), bf),
            pltpu.VMEM((rows, 1024), jnp.float32),
            pltpu.VMEM((rows, 384), bf),
            pltpu.VMEM((rows + 2 * WIN, 768), bf),
            pltpu.VMEM((4, rows, 384), bf),
            pltpu.VMEM((2, 3, sections, wo_rows, 128), bf),
            pltpu.VMEM((4, width, 384), bf),
            pltpu.VMEM((3, 8, 128), jnp.int32),
            pltpu.VMEM((8, 128), jnp.int32),
            dma((sections,)), dma((sections,)), dma((sections,)), dma((shards,)),
            dma((sections,)), dma((sections,)), dma((sections,)), dma((3, sections)), dma, dma,
            dma((2,)), dma((2,)), dma((2,)), dma((2,)),
            dma((blocks,)), dma((blocks,)), dma((blocks,)), dma((3, blocks)),
        ],
        compiler_params=pltpu.CompilerParams(
            collective_id=0, has_side_effects=True, vmem_limit_bytes=52 * 1024 * 1024
        ),
    )(patches, ids, norm_gain[None], pack, bias)


def solution(mesh):
    placed = (
        P(("section", "dp"), None),
        P(("section", "dp")),
        P(),
        P(("section", "dp"), None, "tensor"),
        P(None, "tensor"),
        P(("section", "dp"), "tensor"),
    )
    sections, cores, heads = mesh.shape["section"], mesh.shape["dp"], mesh.shape["tensor"]

    def body(*args):
        patches, w_qkv = args[0], args[3]
        rows, width = patches.shape
        depth = w_qkv.shape[0]
        fits = (
            cores == 2
            and heads == 4
            and sections % 2 == 0
            and depth % 32 == 0
            and w_qkv.shape[2] == 320
            and width % 256 == 0
            and rows == 768
        )
        return fused(sections, *args) if fits else local(*args)

    return jax.shard_map(
        body, mesh=mesh, in_specs=placed, out_specs=P(("section", "dp"), None), check_vma=False
    )
```

```python
import functools
import math

import jax
import jax.numpy as jnp
from jax import lax
from jax.experimental import pallas as pl
from jax.experimental.pallas import tpu as pltpu
from jax.sharding import PartitionSpec as P

HEAD = 80
WIN = 64
MESH = pl.DeviceIdType.MESH


def with_halo(cells, sides, width):
    for axis, dim in sides:
        count = lax.axis_size(axis)
        ends = count - 1
        head = lax.slice_in_dim(cells, 0, width, axis=dim)
        tail = lax.slice_in_dim(cells, cells.shape[dim] - width, cells.shape[dim], axis=dim)
        cells = jnp.concatenate(
            [
                lax.ppermute(tail, axis, [(i, (i + 1) % count) for i in range(ends)]),
                cells,
                lax.ppermute(head, axis, [((i + 1) % count, i) for i in range(ends)]),
            ],
            axis=dim,
        )
    return cells


def local(patches, window_ids, norm_gain, w_qkv, qkv_bias, w_out):
    rows = patches.shape[0]
    local_cols = w_qkv.shape[2]
    local_heads = local_cols // HEAD
    values_f = patches.astype(jnp.float32)
    scale_row = lax.rsqrt(jnp.mean(values_f * values_f, axis=-1, keepdims=True) + 1e-06)
    normed = (values_f * scale_row * norm_gain).astype(jnp.bfloat16)
    piece = lax.all_gather(w_qkv, ("section", "dp"), axis=0, tiled=True)
    count = piece.shape[0]
    proj = jnp.dot(normed, piece.reshape(count, 3 * local_cols), preferred_element_type=jnp.float32)
    proj = (proj + qkv_bias.reshape(3 * local_cols)).astype(jnp.bfloat16)
    keyvals = with_halo(proj[:, local_cols:], ((("section", "dp"), 0),), WIN)
    marks = with_halo(window_ids + 1, ((("section", "dp"), 0),), WIN)
    block_rows = 128
    blocks = rows // block_rows
    key_span = block_rows + 2 * WIN
    queries = proj[:, :local_cols].reshape(blocks, block_rows, local_heads, HEAD)
    kv_blocks = jnp.stack(
        [keyvals[i * block_rows : i * block_rows + key_span] for i in range(blocks)]
    )
    mark_blocks = jnp.stack(
        [marks[i * block_rows : i * block_rows + key_span] for i in range(blocks)]
    )
    keys = kv_blocks[:, :, :local_cols].reshape(blocks, key_span, local_heads, HEAD)
    vals = kv_blocks[:, :, local_cols:].reshape(blocks, key_span, local_heads, HEAD)
    mark_q = marks[WIN : WIN + rows].reshape(blocks, block_rows)
    allowed = mark_q[:, :, None] == mark_blocks[:, None, :]
    factor = 1.0 / HEAD**0.5
    scores = (
        jnp.einsum("bqhd,bkhd->bhqk", queries, keys, preferred_element_type=jnp.float32) * factor
    )
    scores = jnp.where(allowed[:, None], scores, jnp.float32(-1e30))
    top = jnp.max(scores, axis=-1, keepdims=True)
    expo = jnp.where(allowed[:, None], jnp.exp(scores - top), jnp.float32(0.0))
    probs = (expo / jnp.sum(expo, axis=-1, keepdims=True)).astype(jnp.bfloat16)
    attn = jnp.einsum("bhqk,bkhd->bqhd", probs, vals, preferred_element_type=jnp.float32)
    attn = attn.reshape(rows, local_cols).astype(jnp.bfloat16)
    partial_out = lax.dot_general(
        attn,
        lax.all_gather(w_out, ("section", "dp"), axis=0, tiled=True),
        (((1,), (1,)), ((), ())),
        preferred_element_type=jnp.float32,
    )
    summed = lax.psum(partial_out.astype(jnp.bfloat16), "tensor").astype(jnp.float32)
    return (values_f + summed).astype(jnp.bfloat16)


def rot(x, by):
    return pltpu.roll(x.astype(jnp.float32), by, 1).astype(x.dtype)


def kernel(
    sections,
    x_ref, ids_ref, gain_ref, w_ref, wout_ref, bias_ref, out_ref,
    tmp, tmpb, pk, bias, wp, normed, acc, q3, kv3, rbuf, at0, at1, wo, wof, idb, kid,
    up_s, dn_s, sib_s, wp_r, wx_s, wy_s, wf_s, w_r, ws_s, ws_r,
    id_s, id_r, h_s, h_r, ax_s, ay_s, af_s, a_r,
):
    rows, width = x_ref.shape
    depth = width // (2 * sections)
    halfd = depth // 2
    region = ((0, 4 * depth), (4 * depth, 2 * depth + halfd), (6 * depth + halfd, 4 * depth))
    half_at = (0, 2)
    blocks = rows // 128
    last = sections - 1
    bf = jnp.bfloat16
    s, c, t = lax.axis_index("section"), lax.axis_index("dp"), lax.axis_index("tensor")
    oc = 1 - c
    tx = t + 1 - 2 * (t % 2)
    ty = (t + 2) % 4
    td = (tx + 2) % 4
    up, dn, sib = (s + 1, c, t), (s - 1, c, t), (s, oc, t)
    xn, yn = (s, c, tx), (s, c, ty)
    hz = s - 1 + 2 * c
    hdev = (hz, oc, t)
    has_up, has_dn = s < last, s > 0
    has_h = jnp.logical_and(hz >= 0, hz <= last)

    def rc(src, dst, ss, rs, dev):
        return pltpu.make_async_remote_copy(
            src_ref=src, dst_ref=dst, send_sem=ss, recv_sem=rs, device_id=dev, device_id_type=MESH
        )

    barrier = pltpu.get_barrier_semaphore()

    def greet(dev):
        pl.semaphore_signal(barrier, inc=1, device_id=dev, device_id_type=MESH)

    greet(sib)
    greet(xn)
    greet(yn)

    @pl.when(has_up)
    def _():
        greet(up)

    @pl.when(has_dn)
    def _():
        greet(dn)

    @pl.when(has_h)
    def _():
        greet(hdev)

    def lanes(n):
        return lax.broadcasted_iota(jnp.int32, (n, 128), 1)

    def arrange(h, q, k, v):
        n = q[0].shape[0]
        la = lanes(n)
        if h == 0:
            main = [z[0] for z in (q, k, v)]
            rest = (q[1], rot(k[1], 32), rot(v[1], 64))
        else:
            main = [jnp.where(la < 32, z[2], z[1]) for z in (q, k, v)]
            rest = (rot(q[2], 96), k[2], rot(v[2], 32))
        more = jnp.where(la < 32, rest[0], jnp.where(la < 64, rest[1], rest[2]))
        return main + [jnp.where(la < 96, more, jnp.zeros_like(more))]

    def tiles(ref, i):
        return [ref[i, :, 128 * m : 128 * m + 128] for m in range(3)]

    for i in range(3):
        tmp[i, :, 256:384] = jnp.zeros((depth, 128), bf)
        tmp[i, :, 0:320] = w_ref[i]
    tmp[3, :, 256:384] = jnp.zeros((depth, 128), bf)
    tmp[3, :, 0:320] = wout_ref[...]
    qkv = [tiles(tmp, i) for i in range(3)]
    for h in range(2):
        for m, tile in enumerate(arrange(h, *qkv)):
            base = region[half_at[h]][0] + m * depth
            pk[base : base + depth, :] = tile
    w0, w1, w2 = tiles(tmp, 3)
    la = lanes(depth)
    base = region[1][0]
    pk[base : base + depth, :] = w0
    pk[base + depth : base + 2 * depth, :] = jnp.where(la < 32, w2, w1)
    wr = rot(jnp.where(la < 32, w1, w2), 64)
    pk[base + 2 * depth : base + 2 * depth + halfd, :] = jnp.where(
        lanes(halfd) < 64, rot(wr[:halfd], 64), wr[halfd:]
    )
    idb[1] = jnp.zeros((8, 128), jnp.int32)
    idb[1, 0:blocks, :] = ids_ref[...]

    peers = 3 + has_up.astype(jnp.int32) + has_dn.astype(jnp.int32) + has_h.astype(jnp.int32)
    pl.semaphore_wait(barrier, peers)

    def src_of(k, j, own):
        r = pl.ds(*region[k])
        return pk.at[r] if own else wp.at[2 * j + c, r]

    def d_z(sem, dev, k, j, own):
        g = 2 * j + c
        return rc(src_of(k, j, own), wp.at[g, pl.ds(*region[k])], sem.at[k, j], wp_r.at[k, g], dev)

    def d_up(k, j, own=False):
        return d_z(up_s, up, k, j, own)

    def d_dn(k, j, own=False):
        return d_z(dn_s, dn, k, j, own)

    def d_sib(k, j, own=False):
        return d_z(sib_s, sib, k, j, own)

    def got(k, j, parity):
        v = wp.at[2 * j + parity, pl.ds(*region[k])]
        rc(v, v, sib_s.at[k, j], wp_r.at[k, 2 * j + parity], sib).wait_recv()

    def d_wx(j, own=False):
        return rc(src_of(1, j, own), wo.at[c, 0, j], wx_s.at[j], w_r.at[0, j], xn)

    def d_wy(j, own=False):
        return rc(src_of(1, j, own), wo.at[c, 1, j], wy_s.at[j], w_r.at[1, j], yn)

    def d_fx(j):
        return rc(wo.at[c, 0, j], wo.at[c, 2, j], wf_s.at[j], w_r.at[2, j], yn)

    def d_fy(j):
        return rc(wo.at[c, 1, j], wo.at[c, 2, j], wf_s.at[j], w_r.at[2, j], xn)

    def d_ws():
        return rc(wo.at[c], wo.at[c], ws_s, ws_r, sib)

    def start_own(k):
        @pl.when(has_up)
        def _():
            d_up(k, s, True).start()

        @pl.when(has_dn)
        def _():
            d_dn(k, s, True).start()

        d_sib(k, s, True).start()
        if k == 1:
            d_wx(s, True).start()
            d_wy(s, True).start()

    def pass_on(k, d):
        jb, ja = s - d, s + d

        @pl.when(jb >= 0)
        def _():
            got(k, jb, c)

            @pl.when(has_up)
            def _():
                d_up(k, jb).start()

            d_sib(k, jb).start()
            if k == 1:
                d_wx(jb).start()
                d_wy(jb).start()

        @pl.when(ja <= last)
        def _():
            got(k, ja, c)

            @pl.when(has_dn)
            def _():
                d_dn(k, ja).start()

            d_sib(k, ja).start()
            if k == 1:
                d_wx(ja).start()
                d_wy(ja).start()

    start_own(0)
    start_own(1)

    def d_id(k):
        return functools.partial(rc, idb.at[1], idb.at[2 - 2 * k], id_s.at[k], id_r.at[1 - k])

    def to_sides(d):
        for k in range(2):

            @pl.when(c == 1 - k)
            def _():
                d(k)(sib).start()

            @pl.when(jnp.logical_and(c == k, has_h))
            def _():
                d(k)(hdev).start()

    to_sides(d_id)

    tmpb[:, 256:384] = jnp.zeros((8, 128), jnp.float32)
    tmpb[0:3, 0:320] = bias_ref[...]
    bt = [
        [jnp.broadcast_to(tmpb[i : i + 1, 128 * m : 128 * m + 128], (8, 128)) for m in range(3)]
        for i in range(3)
    ]
    for h in range(2):
        bias[h] = jnp.concatenate(arrange(h, *bt), axis=1)

    gain = jnp.concatenate([gain_ref[i : i + 1, :] for i in range(width // 128)], axis=1)

    def norm_block(i, _):
        r = pl.ds(pl.multiple_of(i * 128, 128), 128)
        v = x_ref[r, :].astype(jnp.float32)
        sc = lax.rsqrt(jnp.mean(v * v, axis=-1, keepdims=True) + 1e-06)
        n = v * sc * gain
        for g in range(2 * sections):
            normed[g, r, :] = n[:, g * depth : (g + 1) * depth].astype(bf)
        return 0

    lax.fori_loop(0, blocks, norm_block, 0)

    def mm(h, ref, g):
        a = normed[g]
        base = region[half_at[h]][0]
        for p in range(2):
            lo = ref[pl.ds(base + 2 * p * depth, depth), :]
            hi = ref[pl.ds(base + (2 * p + 1) * depth, depth), :]
            w = jnp.concatenate([lo, hi], axis=1)
            acc[:, 256 * p : 256 * p + 256] += jnp.dot(a, w, preferred_element_type=jnp.float32)

    def mm_own(h):
        acc[...] = jnp.broadcast_to(bias[h, 0:1, :], (rows, 512))
        mm(h, pk, 2 * s + c)
        got(half_at[h], s, oc)
        mm(h, wp.at[2 * s + oc], 2 * s + oc)

    def mm_far(h, d):
        def one(n, _):
            j = jnp.where(n % 2 == 0, s - d, s + d)
            parity = jnp.where(n < 2, c, oc)

            @pl.when(jnp.logical_and(j >= 0, j <= last))
            def _():
                @pl.when(n >= 2)
                def _():
                    got(half_at[h], j, oc)

                mm(h, wp.at[2 * j + parity], 2 * j + parity)

            return 0

        lax.fori_loop(0, 4, one, 0)

    def spread(j):
        rc(wo.at[c, 0, j], wo.at[c, 0, j], wx_s.at[j], w_r.at[0, j], xn).wait_recv()
        rc(wo.at[c, 1, j], wo.at[c, 1, j], wy_s.at[j], w_r.at[1, j], yn).wait_recv()

        @pl.when(j % 2 == 0)
        def _():
            d_fx(j).start()

        @pl.when(j % 2 == 1)
        def _():
            d_fy(j).start()

    def spread_far(d):
        for j in (s - d, s + d):

            @pl.when(jnp.logical_and(j >= 0, j <= last))
            def _():
                spread(j)

    def settle(h):
        def one(i, _):
            r = pl.ds(pl.multiple_of(i * 128, 128), 128)
            rk = pl.ds(pl.multiple_of(i * 128 + WIN, WIN), 128)
            p = acc[r, :]
            q3[h, r, 0:128] = p[:, 0:128].astype(bf)
            q3[h, r, 128:256] = p[:, 384:512].astype(bf)
            kv3[h, rk, 0:128] = p[:, 128:256].astype(bf)
            kv3[h, rk, 128:256] = pltpu.roll(p[:, 384:512], 96, 1).astype(bf)
            kv3[h, rk, 256:512] = p[:, 256:512].astype(bf)
            return 0

        lax.fori_loop(0, blocks, one, 0)

        @pl.when(jnp.logical_and(c == 0, jnp.logical_not(has_h)))
        def _():
            kv3[h, 0:WIN, :] = jnp.zeros((WIN, 512), bf)

        @pl.when(jnp.logical_and(c == 1, jnp.logical_not(has_h)))
        def _():
            kv3[h, rows + WIN : rows + 2 * WIN, :] = jnp.zeros((WIN, 512), bf)

        to_sides(functools.partial(d_h, h))

    def d_h(h, k):
        src = kv3.at[h, pl.ds(WIN if k == 0 else rows, WIN)]
        dst = kv3.at[h, pl.ds(rows + WIN if k == 0 else 0, WIN)]
        return functools.partial(rc, src, dst, h_s.at[h, k], h_r.at[h, 1 - k])

    def wait_sides(d):
        for k in range(2):

            @pl.when(jnp.logical_or(c == 1 - k, has_h))
            def _():
                d(1 - k)(sib).wait_recv()

    lane = lanes(128)
    scale = math.log2(math.e) / HEAD**0.5
    zero = jnp.zeros((128, 128), bf)
    first = (lane < 80, jnp.logical_and(lane >= 32, lane < 112))
    bufs = (at0, at1)

    def d_a(h, tt, b, sem, way, dev):
        v = bufs[h].at[tt, b]
        return rc(v, v, sem.at[h, b], a_r.at[h, way, b], dev)

    def d_af(h, b, by_x):
        return d_a(h, tx, b, af_s, 2, yn) if by_x else d_a(h, ty, b, af_s, 2, xn)

    def attend(h, b):
        r = pl.ds(pl.multiple_of(b * 128, 128), 128)
        rk = pl.ds(pl.multiple_of(b * 128, 128), 256)
        idq = jnp.transpose(jnp.broadcast_to(idb[1, pl.ds(b, 1), :], (128, 128)))
        ok = jnp.concatenate([idq == kid[pl.ds(b, 1), :], idq == kid[pl.ds(b + 1, 1), :]], axis=1)
        qa, qr = q3[h, r, 0:128], q3[h, r, 128:256]
        parts = (
            (jnp.where(first[h], qa, zero), 128),
            (
                jnp.concatenate(
                    [jnp.where(first[h], zero, qa), jnp.where(lane < 32, qr, zero)], axis=1
                ),
                256,
            ),
        )
        outs = []
        for q, span in parts:
            sc = lax.dot_general(
                q, kv3[h, rk, 0:span], (((1,), (1,)), ((), ())), preferred_element_type=jnp.float32
            )
            sc = jnp.where(ok, sc, jnp.float32(-1e30))
            top = jnp.max(sc, axis=-1, keepdims=True)
            e = jnp.exp2((sc - top) * scale)
            total = jnp.sum(e, axis=-1, keepdims=True)
            o = jnp.dot(e.astype(bf), kv3[h, rk, 256 : 256 + span], preferred_element_type=jnp.float32)
            outs.append(o * (1.0 / total))
        o0, o1 = outs
        nil = jnp.float32(0.0)
        bufs[h][t, b, 0:128, :] = jnp.where(first[h], o0, o1[:, :128]).astype(bf)
        more = jnp.where(jnp.logical_and(lane >= 64, lane < 96), o1[:, 128:], nil)
        if h == 0:
            rbuf[r, :] = more
        else:
            both = rbuf[r, :] + pltpu.roll(more, 32, 1)
            la = lanes(64)
            at1[t, b, 128:192, :] = jnp.where(
                la < 64, pltpu.roll(both[:64], 64, 1), both[64:]
            ).astype(bf)
        d_a(h, t, b, ax_s, 0, xn).start()
        d_a(h, t, b, ay_s, 1, yn).start()

    def relay(h, b):
        d_a(h, tx, b, ax_s, 0, xn).wait_recv()
        d_a(h, ty, b, ay_s, 1, yn).wait_recv()

        @pl.when(b % 2 == 0)
        def _():
            d_af(h, b, True).start()

        @pl.when(b % 2 == 1)
        def _():
            d_af(h, b, False).start()

    def order(i):
        return jnp.where(i < blocks - 2, i + 1, jnp.where(i == blocks - 2, 0, blocks - 1))

    def attend_at(h, i):
        @pl.when(i == blocks - 2)
        def _():
            wait_sides(functools.partial(d_h, h))

        attend(h, order(i))

    mm_own(0)

    def step0(d, _):
        pass_on(0, d)

        @pl.when(d == sections // 2)
        def _():
            start_own(2)

        mm_far(0, d)
        pass_on(1, d)
        return 0

    lax.fori_loop(1, sections, step0, 0)
    settle(0)

    @pl.when(jnp.logical_and(c == 0, jnp.logical_not(has_h)))
    def _():
        idb[0] = jnp.full((8, 128), -1, jnp.int32)

    @pl.when(jnp.logical_and(c == 1, jnp.logical_not(has_h)))
    def _():
        idb[2] = jnp.full((8, 128), -1, jnp.int32)

    wait_sides(d_id)
    chain = jnp.concatenate([idb[0, blocks - 1 : blocks], idb[1, 0:blocks], idb[2, 0:1]], axis=0)
    after = jnp.concatenate([chain[1:], chain[:1]], axis=0)
    kid[...] = pltpu.roll(jnp.where(lanes(8) < 64, after, chain), 64, 1)

    mm_own(1)
    spread(s)
    per = -(-blocks // (sections - 1))

    def step1(d, _):
        def some(n, _):
            i = (d - 1) * per + n

            @pl.when(i < blocks)
            def _():
                attend_at(0, i)

                @pl.when(i >= 2)
                def _():
                    relay(0, order(i - 2))

            return 0

        lax.fori_loop(0, per, some, 0)
        pass_on(2, d)
        spread_far(d)
        mm_far(1, d)
        return 0

    lax.fori_loop(1, sections, step1, 0)
    settle(1)

    def attend_step(i, _):
        attend_at(1, i)

        @pl.when(i < 2)
        def _():
            relay(0, order(i + blocks - 2))

        @pl.when(i == 2)
        def _():
            def diag(j, _):
                rc(wo.at[c, 2, j], wo.at[c, 2, j], wf_s.at[j], w_r.at[2, j], xn).wait_recv()
                return 0

            lax.fori_loop(0, sections, diag, 0)
            d_ws().start()

        @pl.when(i >= 2)
        def _():
            relay(1, order(i - 2))

        return 0

    lax.fori_loop(0, blocks, attend_step, 0)

    def other(j, _):
        got(1, j, oc)
        return 0

    lax.fori_loop(0, sections, other, 0)
    rc(wo.at[oc], wo.at[oc], ws_s, ws_r, sib).wait_recv()

    def unpack(src, tt, g):
        at = g * depth
        wof[tt, pl.ds(pl.multiple_of(at, 16), depth), 0:128] = src[0:depth, :]
        wof[tt, pl.ds(pl.multiple_of(at, 16), depth), 128:256] = src[depth : 2 * depth, :]
        h = src[2 * depth : 2 * depth + halfd, :]
        wof[tt, pl.ds(pl.multiple_of(at, 16), halfd), 256:384] = rot(h, 64)
        wof[tt, pl.ds(pl.multiple_of(at + halfd, 16), halfd), 256:384] = h

    def unpack_all(j, _):
        for m in range(2):
            g = 2 * j + m
            for k, tt in enumerate((tx, ty, td)):
                unpack(wo.at[m, k, j], tt, g)

            @pl.when(g != 2 * s + c)
            def _():
                unpack(wp.at[g, pl.ds(*region[1])], t, g)

        return 0

    lax.fori_loop(0, sections, unpack_all, 0)
    unpack(pk.at[pl.ds(*region[1])], t, 2 * s + c)

    def project(i, _):
        @pl.when(i < 2)
        def _():
            relay(1, order(i + blocks - 2))

        b = order(i)
        r = pl.ds(pl.multiple_of(b * 128, 128), 128)
        for h in range(2):
            d_a(h, td, b, af_s, 2, xn).wait_recv()
        parts = []
        for k in range(4):
            f = at1[k, b, 128:192, :].astype(jnp.float32)
            f = jnp.concatenate([pltpu.roll(f, 64, 1), f], axis=0)
            parts += [at0[k, b], at1[k, b, 0:128, :]]
            parts += [jnp.where(lane >= 64, f, jnp.float32(0.0)).astype(bf)]
        a = jnp.concatenate(parts, axis=1)
        for n in range(width // 256):
            w = jnp.concatenate([wof[k, 256 * n : 256 * n + 256, :] for k in range(4)], axis=1)
            total = lax.dot_general(
                a, w, (((1,), (1,)), ((), ())), preferred_element_type=jnp.float32
            )
            cols = slice(256 * n, 256 * n + 256)
            out_ref[r, cols] = (x_ref[r, cols].astype(jnp.float32) + total).astype(bf)
        return 0

    lax.fori_loop(0, blocks, project, 0)

    def sent_w(j, _):
        for k in range(3):

            @pl.when(jnp.logical_and(has_up, j <= s))
            def _():
                d_up(k, j).wait_send()

            @pl.when(jnp.logical_and(has_dn, j >= s))
            def _():
                d_dn(k, j).wait_send()

            d_sib(k, j).wait_send()
        d_wx(j).wait_send()
        d_wy(j).wait_send()
        d_fx(j).wait_send()
        return 0

    lax.fori_loop(0, sections, sent_w, 0)
    d_ws().wait_send()

    def sent_a(b, _):
        for h in range(2):
            d_a(h, t, b, ax_s, 0, xn).wait_send()
            d_a(h, t, b, ay_s, 1, yn).wait_send()
            d_af(h, b, True).wait_send()
        return 0

    lax.fori_loop(0, blocks, sent_a, 0)
    for d in (d_id, functools.partial(d_h, 0), functools.partial(d_h, 1)):
        for k in range(2):

            @pl.when(jnp.logical_or(c == 1 - k, has_h))
            def _():
                d(k)(sib).wait_send()


def fused(sections, patches, window_ids, norm_gain, w_qkv, qkv_bias, w_out):
    rows, width = patches.shape
    depth = w_qkv.shape[0]
    blocks = rows // 128
    bf, f32, dma = jnp.bfloat16, jnp.float32, pltpu.SemaphoreType.DMA
    shards = 2 * sections
    wo_rows = 2 * depth + depth // 2
    pack_rows = 8 * depth + wo_rows
    vmem = pl.BlockSpec(memory_space=pltpu.VMEM)
    return pl.pallas_call(
        functools.partial(kernel, sections),
        out_shape=jax.ShapeDtypeStruct((rows, width), bf),
        in_specs=[vmem] * 6,
        out_specs=vmem,
        scratch_shapes=[
            pltpu.VMEM((4, depth, 384), bf),
            pltpu.VMEM((8, 384), f32),
            pltpu.VMEM((pack_rows, 128), bf),
            pltpu.VMEM((2, 8, 512), f32),
            pltpu.VMEM((shards, pack_rows, 128), bf),
            pltpu.VMEM((shards, rows, depth), bf),
            pltpu.VMEM((rows, 512), f32),
            pltpu.VMEM((2, rows, 256), bf),
            pltpu.VMEM((2, rows + 2 * WIN, 512), bf),
            pltpu.VMEM((rows, 128), f32),
            pltpu.VMEM((4, blocks, 128, 128), bf),
            pltpu.VMEM((4, blocks, 192, 128), bf),
            pltpu.VMEM((2, 3, sections, wo_rows, 128), bf),
            pltpu.VMEM((4, width, 384), bf),
            pltpu.VMEM((3, 8, 128), jnp.int32),
            pltpu.VMEM((8, 128), jnp.int32),
            dma((3, sections)), dma((3, sections)), dma((3, sections)), dma((3, shards)),
            dma((sections,)), dma((sections,)), dma((sections,)), dma((3, sections)), dma, dma,
            dma((2,)), dma((2,)), dma((2, 2)), dma((2, 2)),
            dma((2, blocks)), dma((2, blocks)), dma((2, blocks)), dma((2, 3, blocks)),
        ],
        compiler_params=pltpu.CompilerParams(
            collective_id=0, has_side_effects=True, vmem_limit_bytes=52 * 1024 * 1024
        ),
    )(
        patches,
        window_ids.reshape(blocks, 128),
        norm_gain.reshape(width // 128, 128),
        jnp.transpose(w_qkv, (1, 0, 2)),
        w_out,
        qkv_bias,
    )


def solution(mesh):
    placed = (
        P(("section", "dp"), None),
        P(("section", "dp")),
        P(),
        P(("section", "dp"), None, "tensor"),
        P(None, "tensor"),
        P(("section", "dp"), "tensor"),
    )
    sections, cores, heads = mesh.shape["section"], mesh.shape["dp"], mesh.shape["tensor"]

    def body(*args):
        patches, w_qkv = args[0], args[3]
        rows, width = patches.shape
        depth = w_qkv.shape[0]
        fits = (
            cores == 2
            and heads == 4
            and sections % 2 == 0
            and depth % 32 == 0
            and w_qkv.shape[2] == 320
            and width % 256 == 0
            and rows == 768
        )
        return fused(sections, *args) if fits else local(*args)

    return jax.shard_map(
        body, mesh=mesh, in_specs=placed, out_specs=P(("section", "dp"), None), check_vma=False
    )
```

```python
import functools
import math

import jax
import jax.numpy as jnp
from jax import lax
from jax.experimental import pallas as pl
from jax.experimental.pallas import tpu as pltpu
from jax.sharding import PartitionSpec as P

HEAD = 80
WIN = 64
MESH = pl.DeviceIdType.MESH


def with_halo(cells, sides, width):
    for axis, dim in sides:
        count = lax.axis_size(axis)
        ends = count - 1
        head = lax.slice_in_dim(cells, 0, width, axis=dim)
        tail = lax.slice_in_dim(cells, cells.shape[dim] - width, cells.shape[dim], axis=dim)
        cells = jnp.concatenate(
            [
                lax.ppermute(tail, axis, [(i, (i + 1) % count) for i in range(ends)]),
                cells,
                lax.ppermute(head, axis, [((i + 1) % count, i) for i in range(ends)]),
            ],
            axis=dim,
        )
    return cells


def local(patches, window_ids, norm_gain, w_qkv, qkv_bias, w_out):
    rows = patches.shape[0]
    local_cols = w_qkv.shape[2]
    local_heads = local_cols // HEAD
    values_f = patches.astype(jnp.float32)
    scale_row = lax.rsqrt(jnp.mean(values_f * values_f, axis=-1, keepdims=True) + 1e-06)
    normed = (values_f * scale_row * norm_gain).astype(jnp.bfloat16)
    piece = lax.all_gather(w_qkv, ("section", "dp"), axis=0, tiled=True)
    count = piece.shape[0]
    proj = jnp.dot(normed, piece.reshape(count, 3 * local_cols), preferred_element_type=jnp.float32)
    proj = (proj + qkv_bias.reshape(3 * local_cols)).astype(jnp.bfloat16)
    keyvals = with_halo(proj[:, local_cols:], ((("section", "dp"), 0),), WIN)
    marks = with_halo(window_ids + 1, ((("section", "dp"), 0),), WIN)
    block_rows = 128
    blocks = rows // block_rows
    key_span = block_rows + 2 * WIN
    queries = proj[:, :local_cols].reshape(blocks, block_rows, local_heads, HEAD)
    kv_blocks = jnp.stack(
        [keyvals[i * block_rows : i * block_rows + key_span] for i in range(blocks)]
    )
    mark_blocks = jnp.stack(
        [marks[i * block_rows : i * block_rows + key_span] for i in range(blocks)]
    )
    keys = kv_blocks[:, :, :local_cols].reshape(blocks, key_span, local_heads, HEAD)
    vals = kv_blocks[:, :, local_cols:].reshape(blocks, key_span, local_heads, HEAD)
    mark_q = marks[WIN : WIN + rows].reshape(blocks, block_rows)
    allowed = mark_q[:, :, None] == mark_blocks[:, None, :]
    factor = 1.0 / HEAD**0.5
    scores = (
        jnp.einsum("bqhd,bkhd->bhqk", queries, keys, preferred_element_type=jnp.float32) * factor
    )
    scores = jnp.where(allowed[:, None], scores, jnp.float32(-1e30))
    top = jnp.max(scores, axis=-1, keepdims=True)
    expo = jnp.where(allowed[:, None], jnp.exp(scores - top), jnp.float32(0.0))
    probs = (expo / jnp.sum(expo, axis=-1, keepdims=True)).astype(jnp.bfloat16)
    attn = jnp.einsum("bhqk,bkhd->bqhd", probs, vals, preferred_element_type=jnp.float32)
    attn = attn.reshape(rows, local_cols).astype(jnp.bfloat16)
    partial_out = lax.dot_general(
        attn,
        lax.all_gather(w_out, ("section", "dp"), axis=0, tiled=True),
        (((1,), (1,)), ((), ())),
        preferred_element_type=jnp.float32,
    )
    summed = lax.psum(partial_out.astype(jnp.bfloat16), "tensor").astype(jnp.float32)
    return (values_f + summed).astype(jnp.bfloat16)


def rot(x, by):
    return pltpu.roll(x.astype(jnp.float32), by, 1).astype(x.dtype)


def kernel(
    sections,
    x_in, ids_in, gain_in, w_in, wout_in, bias_in, out_ref,
    x_ref, ids_ref, gain_ref, w_ref, wout_ref, bias_ref, in_s, tmp, tmpb, pk, bias, wp, normed, acc, q3, kv3, rbuf, at0, at1, wo, wof, idb, kid,
    up_s, dn_s, sib_s, wp_r, wx_s, wy_s, wf_s, w_r, ws_s, ws_r,
    id_s, id_r, h_s, h_r, ax_s, ay_s, af_s, a_r,
):
    incoming = [
        pltpu.make_async_copy(a, b, in_s.at[i])
        for i, (a, b) in enumerate(
            (
                (w_in, w_ref), (wout_in, wout_ref), (ids_in, ids_ref),
                (bias_in, bias_ref), (gain_in, gain_ref), (x_in, x_ref),
            )
        )
    ]
    for copy in incoming:
        copy.start()
    rows, width = x_ref.shape
    depth = width // (2 * sections)
    halfd = depth // 2
    region = ((0, 4 * depth), (4 * depth, 2 * depth + halfd), (6 * depth + halfd, 4 * depth))
    half_at = (0, 2)
    blocks = rows // 128
    last = sections - 1
    bf = jnp.bfloat16
    s, c, t = lax.axis_index("section"), lax.axis_index("dp"), lax.axis_index("tensor")
    oc = 1 - c
    tx = t + 1 - 2 * (t % 2)
    ty = (t + 2) % 4
    td = (tx + 2) % 4
    up, dn, sib = (s + 1, c, t), (s - 1, c, t), (s, oc, t)
    xn, yn = (s, c, tx), (s, c, ty)
    hz = s - 1 + 2 * c
    hdev = (hz, oc, t)
    has_up, has_dn = s < last, s > 0
    has_h = jnp.logical_and(hz >= 0, hz <= last)

    def rc(src, dst, ss, rs, dev):
        return pltpu.make_async_remote_copy(
            src_ref=src, dst_ref=dst, send_sem=ss, recv_sem=rs, device_id=dev, device_id_type=MESH
        )

    barrier = pltpu.get_barrier_semaphore()

    def greet(dev):
        pl.semaphore_signal(barrier, inc=1, device_id=dev, device_id_type=MESH)

    greet(sib)
    greet(xn)
    greet(yn)

    @pl.when(has_up)
    def _():
        greet(up)

    @pl.when(has_dn)
    def _():
        greet(dn)

    @pl.when(has_h)
    def _():
        greet(hdev)

    def lanes(n):
        return lax.broadcasted_iota(jnp.int32, (n, 128), 1)

    def arrange(h, q, k, v):
        n = q[0].shape[0]
        la = lanes(n)
        if h == 0:
            main = [z[0] for z in (q, k, v)]
            rest = (q[1], rot(k[1], 32), rot(v[1], 64))
        else:
            main = [jnp.where(la < 32, z[2], z[1]) for z in (q, k, v)]
            rest = (rot(q[2], 96), k[2], rot(v[2], 32))
        more = jnp.where(la < 32, rest[0], jnp.where(la < 64, rest[1], rest[2]))
        return main + [jnp.where(la < 96, more, jnp.zeros_like(more))]

    def tiles(ref, i):
        return [ref[i, :, 128 * m : 128 * m + 128] for m in range(3)]

    for copy in incoming[:3]:
        copy.wait()
    for i in range(3):
        tmp[i, :, 256:384] = jnp.zeros((depth, 128), bf)
        tmp[i, :, 0:320] = w_ref[i]
    tmp[3, :, 256:384] = jnp.zeros((depth, 128), bf)
    tmp[3, :, 0:320] = wout_ref[...]
    qkv = [tiles(tmp, i) for i in range(3)]
    for h in range(2):
        for m, tile in enumerate(arrange(h, *qkv)):
            base = region[half_at[h]][0] + m * depth
            pk[base : base + depth, :] = tile
    w0, w1, w2 = tiles(tmp, 3)
    la = lanes(depth)
    base = region[1][0]
    pk[base : base + depth, :] = w0
    pk[base + depth : base + 2 * depth, :] = jnp.where(la < 32, w2, w1)
    wr = rot(jnp.where(la < 32, w1, w2), 64)
    pk[base + 2 * depth : base + 2 * depth + halfd, :] = jnp.where(
        lanes(halfd) < 64, rot(wr[:halfd], 64), wr[halfd:]
    )
    idb[1] = jnp.zeros((8, 128), jnp.int32)
    idb[1, 0:blocks, :] = ids_ref[...]

    peers = 3 + has_up.astype(jnp.int32) + has_dn.astype(jnp.int32) + has_h.astype(jnp.int32)
    pl.semaphore_wait(barrier, peers)

    def src_of(k, j, own):
        r = pl.ds(*region[k])
        return pk.at[r] if own else wp.at[2 * j + c, r]

    def d_z(sem, dev, k, j, own):
        g = 2 * j + c
        return rc(src_of(k, j, own), wp.at[g, pl.ds(*region[k])], sem.at[k, j], wp_r.at[k, g], dev)

    def d_up(k, j, own=False):
        return d_z(up_s, up, k, j, own)

    def d_dn(k, j, own=False):
        return d_z(dn_s, dn, k, j, own)

    def d_sib(k, j, own=False):
        return d_z(sib_s, sib, k, j, own)

    def got(k, j, parity):
        v = wp.at[2 * j + parity, pl.ds(*region[k])]
        rc(v, v, sib_s.at[k, j], wp_r.at[k, 2 * j + parity], sib).wait_recv()

    def d_wx(j, own=False):
        return rc(src_of(1, j, own), wo.at[c, 0, j], wx_s.at[j], w_r.at[0, j], xn)

    def d_wy(j, own=False):
        return rc(src_of(1, j, own), wo.at[c, 1, j], wy_s.at[j], w_r.at[1, j], yn)

    def d_fx(j):
        return rc(wo.at[c, 0, j], wo.at[c, 2, j], wf_s.at[j], w_r.at[2, j], yn)

    def d_fy(j):
        return rc(wo.at[c, 1, j], wo.at[c, 2, j], wf_s.at[j], w_r.at[2, j], xn)

    def d_ws():
        return rc(wo.at[c], wo.at[c], ws_s, ws_r, sib)

    def start_own(k):
        @pl.when(has_up)
        def _():
            d_up(k, s, True).start()

        @pl.when(has_dn)
        def _():
            d_dn(k, s, True).start()

        d_sib(k, s, True).start()
        if k == 1:
            d_wx(s, True).start()
            d_wy(s, True).start()

    def pass_on(k, d):
        jb, ja = s - d, s + d

        @pl.when(jb >= 0)
        def _():
            got(k, jb, c)

            @pl.when(has_up)
            def _():
                d_up(k, jb).start()

            d_sib(k, jb).start()
            if k == 1:
                d_wx(jb).start()
                d_wy(jb).start()

        @pl.when(ja <= last)
        def _():
            got(k, ja, c)

            @pl.when(has_dn)
            def _():
                d_dn(k, ja).start()

            d_sib(k, ja).start()
            if k == 1:
                d_wx(ja).start()
                d_wy(ja).start()

    start_own(0)
    start_own(1)

    def d_id(k):
        return functools.partial(rc, idb.at[1], idb.at[2 - 2 * k], id_s.at[k], id_r.at[1 - k])

    def to_sides(d):
        for k in range(2):

            @pl.when(c == 1 - k)
            def _():
                d(k)(sib).start()

            @pl.when(jnp.logical_and(c == k, has_h))
            def _():
                d(k)(hdev).start()

    to_sides(d_id)

    for copy in incoming[3:]:
        copy.wait()
    tmpb[:, 256:384] = jnp.zeros((8, 128), jnp.float32)
    tmpb[0:3, 0:320] = bias_ref[...]
    bt = [
        [jnp.broadcast_to(tmpb[i : i + 1, 128 * m : 128 * m + 128], (8, 128)) for m in range(3)]
        for i in range(3)
    ]
    for h in range(2):
        bias[h] = jnp.concatenate(arrange(h, *bt), axis=1)

    gain = jnp.concatenate([gain_ref[i : i + 1, :] for i in range(width // 128)], axis=1)

    def norm_block(i, _):
        r = pl.ds(pl.multiple_of(i * 128, 128), 128)
        v = x_ref[r, :].astype(jnp.float32)
        sc = lax.rsqrt(jnp.mean(v * v, axis=-1, keepdims=True) + 1e-06)
        n = v * sc * gain
        for g in range(2 * sections):
            normed[g, r, :] = n[:, g * depth : (g + 1) * depth].astype(bf)
        return 0

    lax.fori_loop(0, blocks, norm_block, 0)

    def mm(h, ref, g):
        a = normed[g]
        base = region[half_at[h]][0]
        for p in range(2):
            lo = ref[pl.ds(base + 2 * p * depth, depth), :]
            hi = ref[pl.ds(base + (2 * p + 1) * depth, depth), :]
            w = jnp.concatenate([lo, hi], axis=1)
            acc[:, 256 * p : 256 * p + 256] += jnp.dot(a, w, preferred_element_type=jnp.float32)

    def mm_own(h):
        acc[...] = jnp.broadcast_to(bias[h, 0:1, :], (rows, 512))
        mm(h, pk, 2 * s + c)
        got(half_at[h], s, oc)
        mm(h, wp.at[2 * s + oc], 2 * s + oc)

    def mm_far(h, d):
        def one(n, _):
            j = jnp.where(n % 2 == 0, s - d, s + d)
            parity = jnp.where(n < 2, c, oc)

            @pl.when(jnp.logical_and(j >= 0, j <= last))
            def _():
                @pl.when(n >= 2)
                def _():
                    got(half_at[h], j, oc)

                mm(h, wp.at[2 * j + parity], 2 * j + parity)

            return 0

        lax.fori_loop(0, 4, one, 0)

    def spread(j):
        rc(wo.at[c, 0, j], wo.at[c, 0, j], wx_s.at[j], w_r.at[0, j], xn).wait_recv()
        rc(wo.at[c, 1, j], wo.at[c, 1, j], wy_s.at[j], w_r.at[1, j], yn).wait_recv()

        @pl.when(j % 2 == 0)
        def _():
            d_fx(j).start()

        @pl.when(j % 2 == 1)
        def _():
            d_fy(j).start()

    def spread_far(d):
        for j in (s - d, s + d):

            @pl.when(jnp.logical_and(j >= 0, j <= last))
            def _():
                spread(j)

    def settle(h):
        def one(i, _):
            r = pl.ds(pl.multiple_of(i * 128, 128), 128)
            rk = pl.ds(pl.multiple_of(i * 128 + WIN, WIN), 128)
            p = acc[r, :]
            q3[h, r, 0:128] = p[:, 0:128].astype(bf)
            q3[h, r, 128:256] = p[:, 384:512].astype(bf)
            kv3[h, rk, 0:128] = p[:, 128:256].astype(bf)
            kv3[h, rk, 128:256] = pltpu.roll(p[:, 384:512], 96, 1).astype(bf)
            kv3[h, rk, 256:512] = p[:, 256:512].astype(bf)
            return 0

        lax.fori_loop(0, blocks, one, 0)

        @pl.when(jnp.logical_and(c == 0, jnp.logical_not(has_h)))
        def _():
            kv3[h, 0:WIN, :] = jnp.zeros((WIN, 512), bf)

        @pl.when(jnp.logical_and(c == 1, jnp.logical_not(has_h)))
        def _():
            kv3[h, rows + WIN : rows + 2 * WIN, :] = jnp.zeros((WIN, 512), bf)

        to_sides(functools.partial(d_h, h))

    def d_h(h, k):
        src = kv3.at[h, pl.ds(WIN if k == 0 else rows, WIN)]
        dst = kv3.at[h, pl.ds(rows + WIN if k == 0 else 0, WIN)]
        return functools.partial(rc, src, dst, h_s.at[h, k], h_r.at[h, 1 - k])

    def wait_sides(d):
        for k in range(2):

            @pl.when(jnp.logical_or(c == 1 - k, has_h))
            def _():
                d(1 - k)(sib).wait_recv()

    lane = lanes(128)
    scale = math.log2(math.e) / HEAD**0.5
    zero = jnp.zeros((128, 128), bf)
    first = (lane < 80, jnp.logical_and(lane >= 32, lane < 112))
    bufs = (at0, at1)

    def d_a(h, tt, b, sem, way, dev):
        v = bufs[h].at[tt, b]
        return rc(v, v, sem.at[h, b], a_r.at[h, way, b], dev)

    def d_af(h, b, by_x):
        return d_a(h, tx, b, af_s, 2, yn) if by_x else d_a(h, ty, b, af_s, 2, xn)

    def attend(h, b):
        r = pl.ds(pl.multiple_of(b * 128, 128), 128)
        rk = pl.ds(pl.multiple_of(b * 128, 128), 256)
        idq = jnp.transpose(jnp.broadcast_to(idb[1, pl.ds(b, 1), :], (128, 128)))
        ok = jnp.concatenate([idq == kid[pl.ds(b, 1), :], idq == kid[pl.ds(b + 1, 1), :]], axis=1)
        qa, qr = q3[h, r, 0:128], q3[h, r, 128:256]
        parts = (
            (jnp.where(first[h], qa, zero), 128),
            (
                jnp.concatenate(
                    [jnp.where(first[h], zero, qa), jnp.where(lane < 32, qr, zero)], axis=1
                ),
                256,
            ),
        )
        outs = []
        for q, span in parts:
            sc = lax.dot_general(
                q, kv3[h, rk, 0:span], (((1,), (1,)), ((), ())), preferred_element_type=jnp.float32
            )
            sc = jnp.where(ok, sc, jnp.float32(-1e30))
            top = jnp.max(sc, axis=-1, keepdims=True)
            e = jnp.exp2((sc - top) * scale)
            total = jnp.sum(e, axis=-1, keepdims=True)
            o = jnp.dot(e.astype(bf), kv3[h, rk, 256 : 256 + span], preferred_element_type=jnp.float32)
            outs.append(o * (1.0 / total))
        o0, o1 = outs
        nil = jnp.float32(0.0)
        bufs[h][t, b, 0:128, :] = jnp.where(first[h], o0, o1[:, :128]).astype(bf)
        more = jnp.where(jnp.logical_and(lane >= 64, lane < 96), o1[:, 128:], nil)
        if h == 0:
            rbuf[r, :] = more
        else:
            both = rbuf[r, :] + pltpu.roll(more, 32, 1)
            la = lanes(64)
            at1[t, b, 128:192, :] = jnp.where(
                la < 64, pltpu.roll(both[:64], 64, 1), both[64:]
            ).astype(bf)
        d_a(h, t, b, ax_s, 0, xn).start()
        d_a(h, t, b, ay_s, 1, yn).start()

    def relay(h, b):
        d_a(h, tx, b, ax_s, 0, xn).wait_recv()
        d_a(h, ty, b, ay_s, 1, yn).wait_recv()

        @pl.when(b % 2 == 0)
        def _():
            d_af(h, b, True).start()

        @pl.when(b % 2 == 1)
        def _():
            d_af(h, b, False).start()

    def order(i):
        return jnp.where(i < blocks - 2, i + 1, jnp.where(i == blocks - 2, 0, blocks - 1))

    def attend_at(h, i):
        @pl.when(i == blocks - 2)
        def _():
            wait_sides(functools.partial(d_h, h))

        attend(h, order(i))

    mm_own(0)

    def step0(d, _):
        pass_on(0, d)

        @pl.when(d == 1)
        def _():
            start_own(2)

        @pl.when(d < last)
        def _():
            pass_on(1, d)

        mm_far(0, d)

        @pl.when(d == last)
        def _():
            pass_on(1, d)

        @pl.when(d == 1)
        def _():
            spread(s)

        @pl.when(d > 1)
        def _():
            spread_far(d - 1)

        return 0

    lax.fori_loop(1, sections, step0, 0)
    settle(0)

    @pl.when(jnp.logical_and(c == 0, jnp.logical_not(has_h)))
    def _():
        idb[0] = jnp.full((8, 128), -1, jnp.int32)

    @pl.when(jnp.logical_and(c == 1, jnp.logical_not(has_h)))
    def _():
        idb[2] = jnp.full((8, 128), -1, jnp.int32)

    wait_sides(d_id)
    chain = jnp.concatenate([idb[0, blocks - 1 : blocks], idb[1, 0:blocks], idb[2, 0:1]], axis=0)
    after = jnp.concatenate([chain[1:], chain[:1]], axis=0)
    kid[...] = pltpu.roll(jnp.where(lanes(8) < 64, after, chain), 64, 1)

    per = -(-blocks // (sections - 2))

    def each(lo, what):
        def one(n, _):
            i = lo + n

            @pl.when(jnp.logical_and(i >= 0, i < blocks))
            def _():
                what(i)

            return 0

        lax.fori_loop(0, per, one, 0)

    def relay_half0(i):
        relay(0, order(i))

    def step1(d, _):
        @pl.when(d == 1)
        def _():
            mm_own(1)

        @pl.when(d < last)
        def _():
            pass_on(2, d)
            each((d - 1) * per, functools.partial(attend_at, 0))

        @pl.when(d == 1)
        def _():
            spread_far(last)

        each((d - 2) * per, relay_half0)

        @pl.when(d == last)
        def _():
            def diag(j, _):
                rc(wo.at[c, 2, j], wo.at[c, 2, j], wf_s.at[j], w_r.at[2, j], xn).wait_recv()
                return 0

            lax.fori_loop(0, sections, diag, 0)
            d_ws().start()
            pass_on(2, d)

        mm_far(1, d)
        return 0

    lax.fori_loop(1, sections, step1, 0)
    settle(1)

    def unpack(src, tt, g):
        at = g * depth
        wof[tt, pl.ds(pl.multiple_of(at, 16), depth), 0:128] = src[0:depth, :]
        wof[tt, pl.ds(pl.multiple_of(at, 16), depth), 128:256] = src[depth : 2 * depth, :]
        h = src[2 * depth : 2 * depth + halfd, :]
        wof[tt, pl.ds(pl.multiple_of(at, 16), halfd), 256:384] = rot(h, 64)
        wof[tt, pl.ds(pl.multiple_of(at + halfd, 16), halfd), 256:384] = h

    def unpack_all(j, _):
        for m in range(2):
            g = 2 * j + m
            for k, tt in enumerate((tx, ty, td)):
                unpack(wo.at[m, k, j], tt, g)

            @pl.when(g != 2 * s + c)
            def _():
                unpack(wp.at[g, pl.ds(*region[1])], t, g)

        return 0

    def attend_step(i, _):
        attend_at(1, i)

        @pl.when(i >= 2)
        def _():
            relay(1, order(i - 2))

        @pl.when(i == blocks - 1)
        def _():
            def other(j, _):
                got(1, j, oc)
                return 0

            lax.fori_loop(0, sections, other, 0)
            rc(wo.at[oc], wo.at[oc], ws_s, ws_r, sib).wait_recv()
            lax.fori_loop(0, sections, unpack_all, 0)
            unpack(pk.at[pl.ds(*region[1])], t, 2 * s + c)

        return 0

    lax.fori_loop(0, blocks, attend_step, 0)

    def project(i, _):
        @pl.when(i < 2)
        def _():
            relay(1, order(i + blocks - 2))

        b = order(i)
        r = pl.ds(pl.multiple_of(b * 128, 128), 128)
        for h in range(2):
            d_a(h, td, b, af_s, 2, xn).wait_recv()
        parts = []
        for k in range(4):
            f = at1[k, b, 128:192, :].astype(jnp.float32)
            f = jnp.concatenate([pltpu.roll(f, 64, 1), f], axis=0)
            parts += [at0[k, b], at1[k, b, 0:128, :]]
            parts += [jnp.where(lane >= 64, f, jnp.float32(0.0)).astype(bf)]
        a = jnp.concatenate(parts, axis=1)
        for n in range(width // 256):
            w = jnp.concatenate([wof[k, 256 * n : 256 * n + 256, :] for k in range(4)], axis=1)
            total = lax.dot_general(
                a, w, (((1,), (1,)), ((), ())), preferred_element_type=jnp.float32
            )
            cols = slice(256 * n, 256 * n + 256)
            out_ref[r, cols] = (x_ref[r, cols].astype(jnp.float32) + total).astype(bf)
        return 0

    lax.fori_loop(0, blocks, project, 0)

    def sent_w(j, _):
        for k in range(3):

            @pl.when(jnp.logical_and(has_up, j <= s))
            def _():
                d_up(k, j).wait_send()

            @pl.when(jnp.logical_and(has_dn, j >= s))
            def _():
                d_dn(k, j).wait_send()

            d_sib(k, j).wait_send()
        d_wx(j).wait_send()
        d_wy(j).wait_send()
        d_fx(j).wait_send()
        return 0

    lax.fori_loop(0, sections, sent_w, 0)
    d_ws().wait_send()

    def sent_a(b, _):
        for h in range(2):
            d_a(h, t, b, ax_s, 0, xn).wait_send()
            d_a(h, t, b, ay_s, 1, yn).wait_send()
            d_af(h, b, True).wait_send()
        return 0

    lax.fori_loop(0, blocks, sent_a, 0)
    for d in (d_id, functools.partial(d_h, 0), functools.partial(d_h, 1)):
        for k in range(2):

            @pl.when(jnp.logical_or(c == 1 - k, has_h))
            def _():
                d(k)(sib).wait_send()


def fused(sections, patches, window_ids, norm_gain, w_qkv, qkv_bias, w_out):
    rows, width = patches.shape
    depth = w_qkv.shape[0]
    blocks = rows // 128
    bf, f32, dma = jnp.bfloat16, jnp.float32, pltpu.SemaphoreType.DMA
    shards = 2 * sections
    wo_rows = 2 * depth + depth // 2
    pack_rows = 8 * depth + wo_rows
    vmem = pl.BlockSpec(memory_space=pltpu.VMEM)
    return pl.pallas_call(
        functools.partial(kernel, sections),
        out_shape=jax.ShapeDtypeStruct((rows, width), bf),
        in_specs=[pl.BlockSpec(memory_space=pl.ANY)] * 6,
        out_specs=vmem,
        scratch_shapes=[
            pltpu.VMEM((rows, width), bf),
            pltpu.VMEM((blocks, 128), jnp.int32),
            pltpu.VMEM((width // 128, 128), f32),
            pltpu.VMEM((3, depth, 320), bf),
            pltpu.VMEM((depth, 320), bf),
            pltpu.VMEM((3, 320), f32),
            dma((6,)),
            pltpu.VMEM((4, depth, 384), bf),
            pltpu.VMEM((8, 384), f32),
            pltpu.VMEM((pack_rows, 128), bf),
            pltpu.VMEM((2, 8, 512), f32),
            pltpu.VMEM((shards, pack_rows, 128), bf),
            pltpu.VMEM((shards, rows, depth), bf),
            pltpu.VMEM((rows, 512), f32),
            pltpu.VMEM((2, rows, 256), bf),
            pltpu.VMEM((2, rows + 2 * WIN, 512), bf),
            pltpu.VMEM((rows, 128), f32),
            pltpu.VMEM((4, blocks, 128, 128), bf),
            pltpu.VMEM((4, blocks, 192, 128), bf),
            pltpu.VMEM((2, 3, sections, wo_rows, 128), bf),
            pltpu.VMEM((4, width, 384), bf),
            pltpu.VMEM((3, 8, 128), jnp.int32),
            pltpu.VMEM((8, 128), jnp.int32),
            dma((3, sections)), dma((3, sections)), dma((3, sections)), dma((3, shards)),
            dma((sections,)), dma((sections,)), dma((sections,)), dma((3, sections)), dma, dma,
            dma((2,)), dma((2,)), dma((2, 2)), dma((2, 2)),
            dma((2, blocks)), dma((2, blocks)), dma((2, blocks)), dma((2, 3, blocks)),
        ],
        compiler_params=pltpu.CompilerParams(
            collective_id=0, has_side_effects=True, vmem_limit_bytes=60 * 1024 * 1024
        ),
    )(
        patches,
        window_ids.reshape(blocks, 128),
        norm_gain.reshape(width // 128, 128),
        jnp.transpose(w_qkv, (1, 0, 2)),
        w_out,
        qkv_bias,
    )


def solution(mesh):
    placed = (
        P(("section", "dp"), None),
        P(("section", "dp")),
        P(),
        P(("section", "dp"), None, "tensor"),
        P(None, "tensor"),
        P(("section", "dp"), "tensor"),
    )
    sections, cores, heads = mesh.shape["section"], mesh.shape["dp"], mesh.shape["tensor"]

    def body(*args):
        patches, w_qkv = args[0], args[3]
        rows, width = patches.shape
        depth = w_qkv.shape[0]
        fits = (
            cores == 2
            and heads == 4
            and sections >= 4
            and sections % 2 == 0
            and depth % 32 == 0
            and w_qkv.shape[2] == 320
            and width % 256 == 0
            and rows == 768
        )
        return fused(sections, *args) if fits else local(*args)

    return jax.shard_map(
        body, mesh=mesh, in_specs=placed, out_specs=P(("section", "dp"), None), check_vma=False
    )
```

```python
import functools
import math

import jax
import jax.numpy as jnp
from jax import lax
from jax.experimental import pallas as pl
from jax.experimental.pallas import tpu as pltpu
from jax.sharding import PartitionSpec as P

HEAD = 80
WIN = 64
MESH = pl.DeviceIdType.MESH


def with_halo(cells, sides, width):
    for axis, dim in sides:
        count = lax.axis_size(axis)
        ends = count - 1
        head = lax.slice_in_dim(cells, 0, width, axis=dim)
        tail = lax.slice_in_dim(cells, cells.shape[dim] - width, cells.shape[dim], axis=dim)
        cells = jnp.concatenate(
            [
                lax.ppermute(tail, axis, [(i, (i + 1) % count) for i in range(ends)]),
                cells,
                lax.ppermute(head, axis, [((i + 1) % count, i) for i in range(ends)]),
            ],
            axis=dim,
        )
    return cells


def local(patches, window_ids, norm_gain, w_qkv, qkv_bias, w_out):
    rows = patches.shape[0]
    local_cols = w_qkv.shape[2]
    local_heads = local_cols // HEAD
    values_f = patches.astype(jnp.float32)
    scale_row = lax.rsqrt(jnp.mean(values_f * values_f, axis=-1, keepdims=True) + 1e-06)
    normed = (values_f * scale_row * norm_gain).astype(jnp.bfloat16)
    piece = lax.all_gather(w_qkv, ("section", "dp"), axis=0, tiled=True)
    count = piece.shape[0]
    proj = jnp.dot(normed, piece.reshape(count, 3 * local_cols), preferred_element_type=jnp.float32)
    proj = (proj + qkv_bias.reshape(3 * local_cols)).astype(jnp.bfloat16)
    keyvals = with_halo(proj[:, local_cols:], ((("section", "dp"), 0),), WIN)
    marks = with_halo(window_ids + 1, ((("section", "dp"), 0),), WIN)
    block_rows = 128
    blocks = rows // block_rows
    key_span = block_rows + 2 * WIN
    queries = proj[:, :local_cols].reshape(blocks, block_rows, local_heads, HEAD)
    kv_blocks = jnp.stack(
        [keyvals[i * block_rows : i * block_rows + key_span] for i in range(blocks)]
    )
    mark_blocks = jnp.stack(
        [marks[i * block_rows : i * block_rows + key_span] for i in range(blocks)]
    )
    keys = kv_blocks[:, :, :local_cols].reshape(blocks, key_span, local_heads, HEAD)
    vals = kv_blocks[:, :, local_cols:].reshape(blocks, key_span, local_heads, HEAD)
    mark_q = marks[WIN : WIN + rows].reshape(blocks, block_rows)
    allowed = mark_q[:, :, None] == mark_blocks[:, None, :]
    factor = 1.0 / HEAD**0.5
    scores = (
        jnp.einsum("bqhd,bkhd->bhqk", queries, keys, preferred_element_type=jnp.float32) * factor
    )
    scores = jnp.where(allowed[:, None], scores, jnp.float32(-1e30))
    top = jnp.max(scores, axis=-1, keepdims=True)
    expo = jnp.where(allowed[:, None], jnp.exp(scores - top), jnp.float32(0.0))
    probs = (expo / jnp.sum(expo, axis=-1, keepdims=True)).astype(jnp.bfloat16)
    attn = jnp.einsum("bhqk,bkhd->bqhd", probs, vals, preferred_element_type=jnp.float32)
    attn = attn.reshape(rows, local_cols).astype(jnp.bfloat16)
    partial_out = lax.dot_general(
        attn,
        lax.all_gather(w_out, ("section", "dp"), axis=0, tiled=True),
        (((1,), (1,)), ((), ())),
        preferred_element_type=jnp.float32,
    )
    summed = lax.psum(partial_out.astype(jnp.bfloat16), "tensor").astype(jnp.float32)
    return (values_f + summed).astype(jnp.bfloat16)


def rot(x, by):
    return pltpu.roll(x.astype(jnp.float32), by, 1).astype(x.dtype)


def kernel(
    sections,
    x_in, ids_in, gain_in, w_in, wout_in, bias_in, out_ref,
    x_ref, ids_ref, gain_ref, w_ref, wout_ref, bias_ref, in_s, tmp, tmpb, pk, bias, wp, normed, acc, q3, kv3, rbuf, at0, at1, wo, wof, idb, kid,
    up_s, dn_s, sib_s, wp_r, wx_s, wy_s, wf_s, w_r, ws_s, ws_r,
    id_s, id_r, h_s, h_r, ax_s, ay_s, af_s, a_r,
):
    incoming = [
        pltpu.make_async_copy(a, b, in_s.at[i])
        for i, (a, b) in enumerate(
            (
                (w_in, w_ref), (wout_in, wout_ref), (ids_in, ids_ref),
                (bias_in, bias_ref), (gain_in, gain_ref), (x_in, x_ref),
            )
        )
    ]
    for copy in incoming:
        copy.start()
    rows, width = x_ref.shape
    depth = width // (2 * sections)
    halfd = depth // 2
    region = ((0, 4 * depth), (4 * depth, 2 * depth + halfd), (6 * depth + halfd, 4 * depth))
    half_at = (0, 2)
    blocks = rows // 128
    last = sections - 1
    bf = jnp.bfloat16
    s, c, t = lax.axis_index("section"), lax.axis_index("dp"), lax.axis_index("tensor")
    oc = 1 - c
    tx = t + 1 - 2 * (t % 2)
    ty = (t + 2) % 4
    td = (tx + 2) % 4
    up, dn, sib = (s + 1, c, t), (s - 1, c, t), (s, oc, t)
    xn, yn = (s, c, tx), (s, c, ty)
    hz = s - 1 + 2 * c
    hdev = (hz, oc, t)
    has_up, has_dn = s < last, s > 0
    has_h = jnp.logical_and(hz >= 0, hz <= last)

    def rc(src, dst, ss, rs, dev):
        return pltpu.make_async_remote_copy(
            src_ref=src, dst_ref=dst, send_sem=ss, recv_sem=rs, device_id=dev, device_id_type=MESH
        )

    barrier = pltpu.get_barrier_semaphore()

    def greet(dev):
        pl.semaphore_signal(barrier, inc=1, device_id=dev, device_id_type=MESH)

    greet(sib)
    greet(xn)
    greet(yn)

    @pl.when(has_up)
    def _():
        greet(up)

    @pl.when(has_dn)
    def _():
        greet(dn)

    @pl.when(has_h)
    def _():
        greet(hdev)

    def lanes(n):
        return lax.broadcasted_iota(jnp.int32, (n, 128), 1)

    def arrange(h, q, k, v):
        n = q[0].shape[0]
        la = lanes(n)
        if h == 0:
            main = [z[0] for z in (q, k, v)]
            rest = (q[1], rot(k[1], 32), rot(v[1], 64))
        else:
            main = [jnp.where(la < 32, z[2], z[1]) for z in (q, k, v)]
            rest = (rot(q[2], 96), k[2], rot(v[2], 32))
        more = jnp.where(la < 32, rest[0], jnp.where(la < 64, rest[1], rest[2]))
        return main + [jnp.where(la < 96, more, jnp.zeros_like(more))]

    def tiles(ref, i):
        return [ref[i, :, 128 * m : 128 * m + 128] for m in range(3)]

    for copy in incoming[:3]:
        copy.wait()
    for i in range(3):
        tmp[i, :, 256:384] = jnp.zeros((depth, 128), bf)
        tmp[i, :, 0:320] = w_ref[i]
    tmp[3, :, 256:384] = jnp.zeros((depth, 128), bf)
    tmp[3, :, 0:320] = wout_ref[...]
    qkv = [tiles(tmp, i) for i in range(3)]
    for h in range(2):
        for m, tile in enumerate(arrange(h, *qkv)):
            base = region[half_at[h]][0] + m * depth
            pk[base : base + depth, :] = tile
    w0, w1, w2 = tiles(tmp, 3)
    la = lanes(depth)
    base = region[1][0]
    pk[base : base + depth, :] = w0
    pk[base + depth : base + 2 * depth, :] = jnp.where(la < 32, w2, w1)
    wr = rot(jnp.where(la < 32, w1, w2), 64)
    pk[base + 2 * depth : base + 2 * depth + halfd, :] = jnp.where(
        lanes(halfd) < 64, rot(wr[:halfd], 64), wr[halfd:]
    )
    idb[1] = jnp.zeros((8, 128), jnp.int32)
    idb[1, 0:blocks, :] = ids_ref[...]

    peers = 3 + has_up.astype(jnp.int32) + has_dn.astype(jnp.int32) + has_h.astype(jnp.int32)
    pl.semaphore_wait(barrier, peers)

    def src_of(k, j, own):
        r = pl.ds(*region[k])
        return pk.at[r] if own else wp.at[2 * j + c, r]

    def d_z(sem, dev, k, j, own):
        g = 2 * j + c
        return rc(src_of(k, j, own), wp.at[g, pl.ds(*region[k])], sem.at[k, j], wp_r.at[k, g], dev)

    def d_up(k, j, own=False):
        return d_z(up_s, up, k, j, own)

    def d_dn(k, j, own=False):
        return d_z(dn_s, dn, k, j, own)

    def d_sib(k, j, own=False):
        return d_z(sib_s, sib, k, j, own)

    def got(k, j, parity):
        v = wp.at[2 * j + parity, pl.ds(*region[k])]
        rc(v, v, sib_s.at[k, j], wp_r.at[k, 2 * j + parity], sib).wait_recv()

    def d_wx(j, own=False):
        return rc(src_of(1, j, own), wo.at[c, 0, j], wx_s.at[j], w_r.at[0, j], xn)

    def d_wy(j, own=False):
        return rc(src_of(1, j, own), wo.at[c, 1, j], wy_s.at[j], w_r.at[1, j], yn)

    def d_fx(j):
        return rc(wo.at[c, 0, j], wo.at[c, 2, j], wf_s.at[j], w_r.at[2, j], yn)

    def d_fy(j):
        return rc(wo.at[c, 1, j], wo.at[c, 2, j], wf_s.at[j], w_r.at[2, j], xn)

    def d_ws():
        return rc(wo.at[c], wo.at[c], ws_s, ws_r, sib)

    def start_own(k):
        @pl.when(has_up)
        def _():
            d_up(k, s, True).start()

        @pl.when(has_dn)
        def _():
            d_dn(k, s, True).start()

        d_sib(k, s, True).start()
        if k == 1:
            d_wx(s, True).start()
            d_wy(s, True).start()

    def pass_on(k, d):
        jb, ja = s - d, s + d

        @pl.when(jb >= 0)
        def _():
            got(k, jb, c)

            @pl.when(has_up)
            def _():
                d_up(k, jb).start()

            d_sib(k, jb).start()
            if k == 1:
                d_wx(jb).start()
                d_wy(jb).start()

        @pl.when(ja <= last)
        def _():
            got(k, ja, c)

            @pl.when(has_dn)
            def _():
                d_dn(k, ja).start()

            d_sib(k, ja).start()
            if k == 1:
                d_wx(ja).start()
                d_wy(ja).start()

    start_own(0)
    start_own(1)

    def d_id(k):
        return functools.partial(rc, idb.at[1], idb.at[2 - 2 * k], id_s.at[k], id_r.at[1 - k])

    def to_sides(d):
        for k in range(2):

            @pl.when(c == 1 - k)
            def _():
                d(k)(sib).start()

            @pl.when(jnp.logical_and(c == k, has_h))
            def _():
                d(k)(hdev).start()

    to_sides(d_id)

    for copy in incoming[3:]:
        copy.wait()
    tmpb[:, 256:384] = jnp.zeros((8, 128), jnp.float32)
    tmpb[0:3, 0:320] = bias_ref[...]
    bt = [
        [jnp.broadcast_to(tmpb[i : i + 1, 128 * m : 128 * m + 128], (8, 128)) for m in range(3)]
        for i in range(3)
    ]
    for h in range(2):
        bias[h] = jnp.concatenate(arrange(h, *bt), axis=1)

    gain = jnp.concatenate([gain_ref[i : i + 1, :] for i in range(width // 128)], axis=1)

    def norm_block(i, _):
        r = pl.ds(pl.multiple_of(i * 128, 128), 128)
        v = x_ref[r, :].astype(jnp.float32)
        sc = lax.rsqrt(jnp.mean(v * v, axis=-1, keepdims=True) + 1e-06)
        n = v * sc * gain
        for g in range(2 * sections):
            normed[g, r, :] = n[:, g * depth : (g + 1) * depth].astype(bf)
        return 0

    lax.fori_loop(0, blocks, norm_block, 0)

    def mm(h, ref, g):
        a = normed[g]
        base = region[half_at[h]][0]
        for p in range(2):
            lo = ref[pl.ds(base + 2 * p * depth, depth), :]
            hi = ref[pl.ds(base + (2 * p + 1) * depth, depth), :]
            w = jnp.concatenate([lo, hi], axis=1)
            acc[:, 256 * p : 256 * p + 256] += jnp.dot(a, w, preferred_element_type=jnp.float32)

    def mm_own(h):
        acc[...] = jnp.broadcast_to(bias[h, 0:1, :], (rows, 512))
        mm(h, pk, 2 * s + c)
        got(half_at[h], s, oc)
        mm(h, wp.at[2 * s + oc], 2 * s + oc)

    def mm_far(h, d):
        def one(n, _):
            j = jnp.where(n % 2 == 0, s - d, s + d)
            parity = jnp.where(n < 2, c, oc)

            @pl.when(jnp.logical_and(j >= 0, j <= last))
            def _():
                @pl.when(n >= 2)
                def _():
                    got(half_at[h], j, oc)

                mm(h, wp.at[2 * j + parity], 2 * j + parity)

            return 0

        lax.fori_loop(0, 4, one, 0)

    def spread(j):
        rc(wo.at[c, 0, j], wo.at[c, 0, j], wx_s.at[j], w_r.at[0, j], xn).wait_recv()
        rc(wo.at[c, 1, j], wo.at[c, 1, j], wy_s.at[j], w_r.at[1, j], yn).wait_recv()

        @pl.when(j % 2 == 0)
        def _():
            d_fx(j).start()

        @pl.when(j % 2 == 1)
        def _():
            d_fy(j).start()

    def spread_far(d):
        for j in (s - d, s + d):

            @pl.when(jnp.logical_and(j >= 0, j <= last))
            def _():
                spread(j)

    def settle(h):
        def one(i, _):
            r = pl.ds(pl.multiple_of(i * 128, 128), 128)
            rk = pl.ds(pl.multiple_of(i * 128 + WIN, WIN), 128)
            p = acc[r, :]
            q3[h, r, 0:128] = p[:, 0:128].astype(bf)
            q3[h, r, 128:256] = p[:, 384:512].astype(bf)
            kv3[h, rk, 0:128] = p[:, 128:256].astype(bf)
            kv3[h, rk, 128:256] = pltpu.roll(p[:, 384:512], 96, 1).astype(bf)
            kv3[h, rk, 256:512] = p[:, 256:512].astype(bf)
            return 0

        lax.fori_loop(0, blocks, one, 0)

        @pl.when(jnp.logical_and(c == 0, jnp.logical_not(has_h)))
        def _():
            kv3[h, 0:WIN, :] = jnp.zeros((WIN, 512), bf)

        @pl.when(jnp.logical_and(c == 1, jnp.logical_not(has_h)))
        def _():
            kv3[h, rows + WIN : rows + 2 * WIN, :] = jnp.zeros((WIN, 512), bf)

        to_sides(functools.partial(d_h, h))

    def d_h(h, k):
        src = kv3.at[h, pl.ds(WIN if k == 0 else rows, WIN)]
        dst = kv3.at[h, pl.ds(rows + WIN if k == 0 else 0, WIN)]
        return functools.partial(rc, src, dst, h_s.at[h, k], h_r.at[h, 1 - k])

    def wait_sides(d):
        for k in range(2):

            @pl.when(jnp.logical_or(c == 1 - k, has_h))
            def _():
                d(1 - k)(sib).wait_recv()

    lane = lanes(128)
    scale = math.log2(math.e) / HEAD**0.5
    zero = jnp.zeros((128, 128), bf)
    first = (lane < 80, jnp.logical_and(lane >= 32, lane < 112))
    bufs = (at0, at1)

    def d_a(h, tt, b, sem, way, dev):
        v = bufs[h].at[tt, b]
        return rc(v, v, sem.at[h, b], a_r.at[h, way, b], dev)

    def d_af(h, b, by_x):
        return d_a(h, tx, b, af_s, 2, yn) if by_x else d_a(h, ty, b, af_s, 2, xn)

    def attend(h, b):
        r = pl.ds(pl.multiple_of(b * 128, 128), 128)
        rk = pl.ds(pl.multiple_of(b * 128, 128), 256)
        idq = jnp.transpose(jnp.broadcast_to(idb[1, pl.ds(b, 1), :], (128, 128)))
        ok = jnp.concatenate([idq == kid[pl.ds(b, 1), :], idq == kid[pl.ds(b + 1, 1), :]], axis=1)
        qa, qr = q3[h, r, 0:128], q3[h, r, 128:256]
        parts = (
            (jnp.where(first[h], qa, zero), 128),
            (
                jnp.concatenate(
                    [jnp.where(first[h], zero, qa), jnp.where(lane < 32, qr, zero)], axis=1
                ),
                256,
            ),
        )
        outs = []
        for q, span in parts:
            sc = lax.dot_general(
                q, kv3[h, rk, 0:span], (((1,), (1,)), ((), ())), preferred_element_type=jnp.float32
            )
            sc = jnp.where(ok, sc, jnp.float32(-1e30))
            top = jnp.max(sc, axis=-1, keepdims=True)
            e = jnp.exp2((sc - top) * scale)
            total = jnp.sum(e, axis=-1, keepdims=True)
            o = jnp.dot(e.astype(bf), kv3[h, rk, 256 : 256 + span], preferred_element_type=jnp.float32)
            outs.append(o * (1.0 / total))
        o0, o1 = outs
        nil = jnp.float32(0.0)
        bufs[h][t, b, 0:128, :] = jnp.where(first[h], o0, o1[:, :128]).astype(bf)
        more = jnp.where(jnp.logical_and(lane >= 64, lane < 96), o1[:, 128:], nil)
        if h == 0:
            rbuf[r, :] = more
        else:
            both = rbuf[r, :] + pltpu.roll(more, 32, 1)
            la = lanes(64)
            at1[t, b, 128:192, :] = jnp.where(
                la < 64, pltpu.roll(both[:64], 64, 1), both[64:]
            ).astype(bf)
        d_a(h, t, b, ax_s, 0, xn).start()
        d_a(h, t, b, ay_s, 1, yn).start()

    def relay(h, b):
        d_a(h, tx, b, ax_s, 0, xn).wait_recv()
        d_a(h, ty, b, ay_s, 1, yn).wait_recv()

        @pl.when(b % 2 == 0)
        def _():
            d_af(h, b, True).start()

        @pl.when(b % 2 == 1)
        def _():
            d_af(h, b, False).start()

    def order(i):
        return jnp.where(i < blocks - 2, i + 1, jnp.where(i == blocks - 2, 0, blocks - 1))

    def attend_at(h, i):
        @pl.when(i == blocks - 2)
        def _():
            wait_sides(functools.partial(d_h, h))

        attend(h, order(i))

    mm_own(0)

    def step0(d, _):
        pass_on(0, d)

        @pl.when(d == 1)
        def _():
            start_own(2)

        @pl.when(d < last)
        def _():
            pass_on(1, d)

        mm_far(0, d)

        @pl.when(d == last)
        def _():
            pass_on(1, d)

        @pl.when(d == 1)
        def _():
            spread(s)

        @pl.when(d > 1)
        def _():
            spread_far(d - 1)

        return 0

    lax.fori_loop(1, sections, step0, 0)
    settle(0)

    @pl.when(jnp.logical_and(c == 0, jnp.logical_not(has_h)))
    def _():
        idb[0] = jnp.full((8, 128), -1, jnp.int32)

    @pl.when(jnp.logical_and(c == 1, jnp.logical_not(has_h)))
    def _():
        idb[2] = jnp.full((8, 128), -1, jnp.int32)

    wait_sides(d_id)
    chain = jnp.concatenate([idb[0, blocks - 1 : blocks], idb[1, 0:blocks], idb[2, 0:1]], axis=0)
    after = jnp.concatenate([chain[1:], chain[:1]], axis=0)
    kid[...] = pltpu.roll(jnp.where(lanes(8) < 64, after, chain), 64, 1)

    per = -(-blocks // (sections - 2))

    def each(lo, what):
        def one(n, _):
            i = lo + n

            @pl.when(jnp.logical_and(i >= 0, i < blocks))
            def _():
                what(i)

            return 0

        lax.fori_loop(0, per, one, 0)

    def relay_half0(i):
        relay(0, order(i))

    def step1(d, _):
        @pl.when(d == 1)
        def _():
            mm_own(1)

        @pl.when(d < last)
        def _():
            pass_on(2, d)
            each((d - 1) * per, functools.partial(attend_at, 0))

        @pl.when(d == 1)
        def _():
            spread_far(last)

        each((d - 2) * per, relay_half0)

        @pl.when(d == last)
        def _():
            pass_on(2, d)

            def diag(j, _):
                rc(wo.at[c, 2, j], wo.at[c, 2, j], wf_s.at[j], w_r.at[2, j], xn).wait_recv()
                return 0

            lax.fori_loop(0, sections, diag, 0)
            d_ws().start()

        mm_far(1, d)
        return 0

    lax.fori_loop(1, sections, step1, 0)
    settle(1)

    def unpack(src, tt, g):
        at = g * depth
        wof[tt, pl.ds(pl.multiple_of(at, 16), depth), 0:128] = src[0:depth, :]
        wof[tt, pl.ds(pl.multiple_of(at, 16), depth), 128:256] = src[depth : 2 * depth, :]
        h = src[2 * depth : 2 * depth + halfd, :]
        wof[tt, pl.ds(pl.multiple_of(at, 16), halfd), 256:384] = rot(h, 64)
        wof[tt, pl.ds(pl.multiple_of(at + halfd, 16), halfd), 256:384] = h

    def unpack_all(j, _):
        for m in range(2):
            g = 2 * j + m
            for k, tt in enumerate((tx, ty, td)):
                unpack(wo.at[m, k, j], tt, g)

            @pl.when(g != 2 * s + c)
            def _():
                unpack(wp.at[g, pl.ds(*region[1])], t, g)

        return 0

    def attend_step(i, _):
        attend_at(1, i)

        @pl.when(i >= 2)
        def _():
            relay(1, order(i - 2))

        @pl.when(i == blocks - 1)
        def _():
            def other(j, _):
                got(1, j, oc)
                return 0

            lax.fori_loop(0, sections, other, 0)
            rc(wo.at[oc], wo.at[oc], ws_s, ws_r, sib).wait_recv()
            lax.fori_loop(0, sections, unpack_all, 0)
            unpack(pk.at[pl.ds(*region[1])], t, 2 * s + c)

        return 0

    lax.fori_loop(0, blocks, attend_step, 0)

    def project(i, _):
        @pl.when(i < 2)
        def _():
            relay(1, order(i + blocks - 2))

        b = order(i)
        r = pl.ds(pl.multiple_of(b * 128, 128), 128)
        for h in range(2):
            d_a(h, td, b, af_s, 2, xn).wait_recv()
        parts = []
        for k in range(4):
            f = at1[k, b, 128:192, :].astype(jnp.float32)
            f = jnp.concatenate([pltpu.roll(f, 64, 1), f], axis=0)
            parts += [at0[k, b], at1[k, b, 0:128, :]]
            parts += [jnp.where(lane >= 64, f, jnp.float32(0.0)).astype(bf)]
        a = jnp.concatenate(parts, axis=1)
        for n in range(width // 256):
            w = jnp.concatenate([wof[k, 256 * n : 256 * n + 256, :] for k in range(4)], axis=1)
            total = lax.dot_general(
                a, w, (((1,), (1,)), ((), ())), preferred_element_type=jnp.float32
            )
            cols = slice(256 * n, 256 * n + 256)
            out_ref[r, cols] = (x_ref[r, cols].astype(jnp.float32) + total).astype(bf)
        return 0

    lax.fori_loop(0, blocks, project, 0)

    def sent_w(j, _):
        for k in range(3):

            @pl.when(jnp.logical_and(has_up, j <= s))
            def _():
                d_up(k, j).wait_send()

            @pl.when(jnp.logical_and(has_dn, j >= s))
            def _():
                d_dn(k, j).wait_send()

            d_sib(k, j).wait_send()
        d_wx(j).wait_send()
        d_wy(j).wait_send()
        d_fx(j).wait_send()
        return 0

    lax.fori_loop(0, sections, sent_w, 0)
    d_ws().wait_send()

    def sent_a(b, _):
        for h in range(2):
            d_a(h, t, b, ax_s, 0, xn).wait_send()
            d_a(h, t, b, ay_s, 1, yn).wait_send()
            d_af(h, b, True).wait_send()
        return 0

    lax.fori_loop(0, blocks, sent_a, 0)
    for d in (d_id, functools.partial(d_h, 0), functools.partial(d_h, 1)):
        for k in range(2):

            @pl.when(jnp.logical_or(c == 1 - k, has_h))
            def _():
                d(k)(sib).wait_send()


def fused(sections, patches, window_ids, norm_gain, w_qkv, qkv_bias, w_out):
    rows, width = patches.shape
    depth = w_qkv.shape[0]
    blocks = rows // 128
    bf, f32, dma = jnp.bfloat16, jnp.float32, pltpu.SemaphoreType.DMA
    shards = 2 * sections
    wo_rows = 2 * depth + depth // 2
    pack_rows = 8 * depth + wo_rows
    vmem = pl.BlockSpec(memory_space=pltpu.VMEM)
    return pl.pallas_call(
        functools.partial(kernel, sections),
        out_shape=jax.ShapeDtypeStruct((rows, width), bf),
        in_specs=[pl.BlockSpec(memory_space=pl.ANY)] * 6,
        out_specs=vmem,
        scratch_shapes=[
            pltpu.VMEM((rows, width), bf),
            pltpu.VMEM((blocks, 128), jnp.int32),
            pltpu.VMEM((width // 128, 128), f32),
            pltpu.VMEM((3, depth, 320), bf),
            pltpu.VMEM((depth, 320), bf),
            pltpu.VMEM((3, 320), f32),
            dma((6,)),
            pltpu.VMEM((4, depth, 384), bf),
            pltpu.VMEM((8, 384), f32),
            pltpu.VMEM((pack_rows, 128), bf),
            pltpu.VMEM((2, 8, 512), f32),
            pltpu.VMEM((shards, pack_rows, 128), bf),
            pltpu.VMEM((shards, rows, depth), bf),
            pltpu.VMEM((rows, 512), f32),
            pltpu.VMEM((2, rows, 256), bf),
            pltpu.VMEM((2, rows + 2 * WIN, 512), bf),
            pltpu.VMEM((rows, 128), f32),
            pltpu.VMEM((4, blocks, 128, 128), bf),
            pltpu.VMEM((4, blocks, 192, 128), bf),
            pltpu.VMEM((2, 3, sections, wo_rows, 128), bf),
            pltpu.VMEM((4, width, 384), bf),
            pltpu.VMEM((3, 8, 128), jnp.int32),
            pltpu.VMEM((8, 128), jnp.int32),
            dma((3, sections)), dma((3, sections)), dma((3, sections)), dma((3, shards)),
            dma((sections,)), dma((sections,)), dma((sections,)), dma((3, sections)), dma, dma,
            dma((2,)), dma((2,)), dma((2, 2)), dma((2, 2)),
            dma((2, blocks)), dma((2, blocks)), dma((2, blocks)), dma((2, 3, blocks)),
        ],
        compiler_params=pltpu.CompilerParams(
            collective_id=0, has_side_effects=True, vmem_limit_bytes=60 * 1024 * 1024
        ),
    )(
        patches,
        window_ids.reshape(blocks, 128),
        norm_gain.reshape(width // 128, 128),
        jnp.transpose(w_qkv, (1, 0, 2)),
        w_out,
        qkv_bias,
    )


def solution(mesh):
    placed = (
        P(("section", "dp"), None),
        P(("section", "dp")),
        P(),
        P(("section", "dp"), None, "tensor"),
        P(None, "tensor"),
        P(("section", "dp"), "tensor"),
    )
    sections, cores, heads = mesh.shape["section"], mesh.shape["dp"], mesh.shape["tensor"]

    def body(*args):
        patches, w_qkv = args[0], args[3]
        rows, width = patches.shape
        depth = w_qkv.shape[0]
        fits = (
            cores == 2
            and heads == 4
            and sections >= 4
            and sections % 2 == 0
            and depth % 32 == 0
            and w_qkv.shape[2] == 320
            and width % 256 == 0
            and rows == 768
        )
        return fused(sections, *args) if fits else local(*args)

    return jax.shard_map(
        body, mesh=mesh, in_specs=placed, out_specs=P(("section", "dp"), None), check_vma=False
    )
```
